512 devices in a mesh: grp: 16 (over y, core), sp: 32 (over x, z).
Axes of the slice: x: 4, y: 8, z: 8, core: 2. Of those that a mesh axis runs over, the one named last changes fastest.
Arguments:
- coarse_latent: bfloat16 [16, 32, 16, 512], P(None, 'sp', 'grp'), may hold values from -6 to 6
- renoise: bfloat16 [8192, 2048], P(('grp', 'sp')), may hold values from -6 to 6
- clip_frames: int32 [16, 4], P('grp'), may hold values from 1 to 16, 32 in all within a row
- patch_embed: bfloat16 [64, 1536], replicated, may hold values from -0.75 to 0.75
- mod_shift: float32 [16, 1536], P('grp'), may hold values from -3 to 3
- mod_scale: float32 [16, 1536], P('grp'), may hold values from 0.25 to 1.75
- qkv_weight: bfloat16 [1536, 2304], P(('grp', 'sp')), may hold values from -0.15625 to 0.15625
- out_weight: bfloat16 [1536, 768], P(('grp', 'sp')), may hold values from -1.75 to 1.75
- q_gain: float32 [768], replicated, may hold values from 0.5 to 18
- k_gain: float32 [768], replicated, may hold values from 0.5 to 18
Outputs:
- updated: bfloat16 [262144, 1536], P(('grp', 'sp'))
The draws below stay inside these ranges and needn't reach their ends.
All inputs are finite; a program needn't handle non-finite values.
Results may differ from the reference program's by a relative error of at most 0.034.
Values may be sent and summed in bfloat16 or wider, within the bound.
A program may use at most 64 MiB of HBM per device.

```python
import math
import jax
import jax.numpy as jnp
import numpy as np
from jax import lax

D = 1536
HEADS = 12
HEAD = 64
C = 16
FH = 16
FW = 32
CLIPS = 4
PATCH = 64
HD = 768
MOST = 16
N_GRP = 16
N_SP = 32


def draw_q_gain(key, part):
    key = jax.random.fold_in(key, 11)
    base = jnp.exp(jax.random.uniform(key, (HEADS, HEAD), jnp.float32, math.log(0.5), math.log(3.0)))
    return base.reshape(HEADS * HEAD)


def draw_k_gain(key, part):
    key = jax.random.fold_in(key, 13)
    base = jnp.exp(jax.random.uniform(key, (HEADS, HEAD), jnp.float32, math.log(0.5), math.log(3.0)))
    return base.reshape(HEADS * HEAD)


def shard_levels(rng, dims, split, low, top_value):
    level = 1.0
    for axis_at, parts in split:
        heights = jax.random.uniform(jax.random.fold_in(jax.random.fold_in(rng, 6), axis_at), (parts,), jnp.float32, low / len(split), top_value / len(split))
        level = level * jnp.repeat(jnp.exp(heights), dims[axis_at] // parts).reshape((-1,) + (1,) * (len(dims) - 1 - axis_at))
    return level


def profile(number_of, total, reach, slope):
    loads = [(1 << 20) // math.isqrt(grade ** slope) + 1 for grade in range(2, number_of + 1)]
    spare, given = total - reach - (number_of - 1), [1] * (number_of - 1)
    while spare > 0:
        free = [i for i in range(number_of - 1) if given[i] < reach]
        whole, left = sum([loads[i] for i in free]), spare
        for i in free:
            more = min(reach - given[i], max(1, left * loads[i] // whole), spare)
            given[i] = given[i] + more
            spare = spare - more
    return np.array([reach] + given)


def ragged_sizes(key, count, total, bound, slope):
    if count == 2:
        one = jax.random.randint(key, (), max(1, total - bound), min(bound, total - 1) + 1)
        return jnp.stack([one, total - one])
    tallies = jnp.asarray(profile(count, total, bound, slope), jnp.int32)
    couples = (count - 1) // 2
    giver, receiver = tallies[1:1 + 2 * couples:2], tallies[2:2 + 2 * couples:2]
    slack = jnp.minimum(giver - 1, bound - receiver)
    moved = jax.random.randint(jax.random.fold_in(key, 1), (couples,), 0, 1 << 20) % (slack + 1)
    tallies = tallies.at[1:1 + 2 * couples:2].set(giver - moved).at[2:2 + 2 * couples:2].set(receiver + moved)
    return tallies[jax.random.permutation(jax.random.fold_in(key, 2), count)]


def scatter_about(key, dims, scale, bound, cuts=(), kind=jnp.bfloat16):
    gain = shard_levels(key, dims, cuts, -0.22, 0.18) if cuts else 1.0
    array = jax.random.normal(key, dims, jnp.float32) * scale * gain
    return jnp.minimum(jnp.maximum(array, -bound), bound).astype(kind)


def setup_inputs(seed: int = 0) -> dict:
    arg_keys = jax.random.split(jax.random.key(seed), 11)
    return {
        "coarse_latent": scatter_about(arg_keys[0], (N_GRP, N_SP, FH, FW * C), 1.0, 6.0, ((1, 32), (2, 16))),
        "renoise": scatter_about(arg_keys[1], (N_GRP * N_SP * FH, FW * PATCH), 1.0, 6.0, ((0, 512),)),
        "clip_frames": jax.vmap(lambda own: ragged_sizes(own, CLIPS, N_SP, MOST, 2))(jax.random.split(arg_keys[2], N_GRP)).reshape((N_GRP, CLIPS)).astype(jnp.int32),
        "patch_embed": scatter_about(arg_keys[3], (PATCH, D), PATCH ** -0.5, 0.75),
        "mod_shift": scatter_about(arg_keys[4], (N_GRP, D), 0.5, 3.0, ((0, 16),), jnp.float32),
        "mod_scale": jnp.clip(1.0 + 0.15 * jax.random.normal(arg_keys[5], (N_GRP, D), jnp.float32), 0.25, 1.75),
        "qkv_weight": scatter_about(arg_keys[6], (D, 3 * HD), D ** -0.5, 0.15625, ((0, 512),)),
        "out_weight": scatter_about(arg_keys[7], (D, HD), (max(HD // 64, 2)) ** -0.5, 1.75, ((0, 512),)),
        "q_gain": draw_q_gain(jax.random.fold_in(arg_keys[10], 71), 0),
        "k_gain": draw_k_gain(jax.random.fold_in(arg_keys[10], 71), 0),
    }


signal_coef = 0.8
noise_coef = 0.6
epsilon = 1e-06

def head_norm(flat_rows, gains):
    shaped = flat_rows.reshape(flat_rows.shape[0], HEADS, HEAD)
    inverse = lax.rsqrt(lax.optimization_barrier(jnp.mean(shaped * shaped, axis=2, keepdims=True)) + epsilon)
    return (shaped * inverse * gains.reshape(1, HEADS, HEAD)).reshape(flat_rows.shape[0], HEADS * HEAD)

def clip_ids(counts, frames):
    ends = jnp.cumsum(counts)
    positions = jnp.arange(frames, dtype=jnp.int32)
    return lax.optimization_barrier(jnp.sum((positions[:, None] >= ends[None, :]).astype(jnp.int32), axis=1))

def temporal(query, keys_all, values_all, same_clip):
    frames, count = (query.shape[0], query.shape[1])
    q_four = query.reshape(frames, count, HEADS, HEAD).astype(jnp.float32)
    k_four = keys_all.reshape(frames, count, HEADS, HEAD).astype(jnp.float32)
    v_four = values_all.reshape(frames, count, HEADS, HEAD).astype(jnp.float32)
    scores = jnp.einsum('fphd,gphd->phfg', q_four, k_four) / math.sqrt(HEAD)
    scores = jnp.where(same_clip[None, None], scores, -jnp.inf)
    top = lax.optimization_barrier(jnp.max(scores, axis=3, keepdims=True))
    expo = jnp.exp(scores - top)
    probs = (expo / lax.optimization_barrier(jnp.sum(expo, axis=3, keepdims=True))).astype(jnp.bfloat16)
    mixed = jnp.einsum('phfg,gphd->fphd', probs.astype(jnp.float32), v_four).astype(jnp.bfloat16)
    return mixed.reshape(frames, count, HEADS * HEAD)

def reference(coarse_latent, renoise, clip_frames, patch_embed, mod_shift, mod_scale, qkv_weight, out_weight, q_gain, k_gain):
    width = HEADS * HEAD
    frame_tokens = FH * FW
    group_tokens = N_SP * frame_tokens

    def one_group(inputs):
        coarse, noise, counts, shift, scale = inputs
        pixels = coarse.reshape(N_SP, FH, FW, 1, C).astype(jnp.float32)
        upsampled = jnp.broadcast_to(pixels, (N_SP, FH, FW, 4, C)).reshape(group_tokens, 4 * C)
        patches = (signal_coef * upsampled + noise_coef * noise.astype(jnp.float32)).astype(jnp.bfloat16)
        hidden = jnp.dot(patches, patch_embed, preferred_element_type=jnp.float32).astype(jnp.bfloat16)
        hidden_f = hidden.astype(jnp.float32)
        row_mean = lax.optimization_barrier(jnp.mean(hidden_f, axis=1, keepdims=True))
        centered = hidden_f - row_mean
        row_var = lax.optimization_barrier(jnp.mean(centered * centered, axis=1, keepdims=True))
        normed = (centered * lax.rsqrt(row_var + epsilon) * scale[None, :] + shift[None, :]).astype(jnp.bfloat16)
        qkv = jnp.dot(normed, qkv_weight, preferred_element_type=jnp.float32)
        query = head_norm(qkv[:, :width], q_gain).astype(jnp.bfloat16)
        keys_all = head_norm(qkv[:, width:2 * width], k_gain).astype(jnp.bfloat16)
        values_all = qkv[:, 2 * width:].astype(jnp.bfloat16)
        segment = clip_ids(counts, N_SP)
        same_clip = segment[:, None] == segment[None, :]
        mixed = temporal(query.reshape(N_SP, frame_tokens, width), keys_all.reshape(N_SP, frame_tokens, width), values_all.reshape(N_SP, frame_tokens, width), same_clip).reshape(group_tokens, width)
        attn = lax.dot_general(mixed, out_weight, (((1,), (1,)), ((), ())), preferred_element_type=jnp.float32)
        return (hidden_f + attn).astype(jnp.bfloat16)
    noise_groups = renoise.reshape(N_GRP, group_tokens, 4 * C)
    result = lax.map(one_group, (coarse_latent, noise_groups, clip_frames, mod_shift, mod_scale))
    return result.reshape(N_GRP * group_tokens, D)
```

```python
import jax
import jax.numpy as jnp
from jax import lax
from jax.experimental import pallas as pl
from jax.experimental.pallas import tpu as pltpu
from jax.sharding import PartitionSpec as P

HEADS = 12
HEAD = 64
C = 16
FH = 16
FW = 32
D = 1536
HD = HEADS * HEAD
TOKENS = FH * FW
N_GRP = 16
N_Y = 8
N_SP = 32
BLOCKS = 3 * HD // 128
PAIRS = HEADS // 2
ROWS = 80
PLANE_ROWS = 96

signal_coef = 0.8
noise_coef = 0.6
epsilon = 1e-06
MESH = pl.DeviceIdType.MESH
F32 = jnp.float32
BF16 = jnp.bfloat16


def iota(shape, axis):
    return lax.broadcasted_iota(jnp.int32, shape, axis)


def dot(a, b):
    return jnp.dot(a, b, preferred_element_type=F32)


def dot_t(a, b):
    return lax.dot_general(a, b, (((1,), (1,)), ((), ())), preferred_element_type=F32)


def one_hot(condition):
    return jnp.where(condition, 1.0, 0.0).astype(BF16)


def kernel(
    coarse_ref,
    noise_ref,
    clip_ref,
    embed_ref,
    shift_ref,
    scale_ref,
    w_ref,
    o_ref,
    qg_ref,
    kg_ref,
    out_ref,
    c_recv,
    w_tiles,
    w_cols,
    factors,
    m_own,
    m_all,
    patches,
    z_send,
    z_recv,
    o_tiles,
    o_all,
    perm,
    mixed_rt,
    mixed_tr,
    returned,
    padded_embed,
    hidden,
    c_ss,
    c_rs,
    w_ss,
    w_rs,
    y_ss,
    y_rs,
    d_ss,
    d_rs,
    m_ss,
    m_rs,
    z_ss,
    z_rs,
    p_ss,
    p_rs,
    oy_ss,
    oy_rs,
    od_ss,
    od_rs,
    r_ss,
    r_rs,
):
    g = lax.axis_index("grp")
    s = lax.axis_index("sp")
    y = g // 2
    core = lax.rem(g, 2)
    sibling = g + 1 - 2 * core
    block = (9 * s + 8) // 16
    owner = (16 * block) // 9 == s

    def sp_peer(j):
        return lax.rem(s + j, N_SP)

    def grp_peer(j):
        return lax.rem(g + j, N_GRP)

    def y_peer(j):
        return lax.rem(y + j, N_Y)

    def owner_of(b):
        return (16 * b) // 9

    def remote(src, dst, send_sem, recv_sem, to):
        return pltpu.make_async_remote_copy(
            src_ref=src,
            dst_ref=dst,
            send_sem=send_sem,
            recv_sem=recv_sem,
            device_id=to,
            device_id_type=MESH,
        )

    def loop(start, stop, body):
        def step(j, carry):
            body(j)
            return carry

        lax.fori_loop(start, stop, step, 0)

    def c_copy(to, slot):
        return remote(
            coarse_ref.at[to], c_recv.at[slot], c_ss.at[to], c_rs.at[slot], (to, s)
        )

    def w_copy(b, slot):
        return remote(
            w_ref.at[:, pl.ds(pl.multiple_of(b * 128, 128), 128)],
            w_tiles.at[slot],
            w_ss.at[b],
            w_rs.at[slot],
            (g, owner_of(b)),
        )

    def y_copy(to, slot):
        return remote(
            w_cols.at[y, core], w_cols.at[slot, core], y_ss.at[to], y_rs.at[slot], (2 * to + core, s)
        )

    def d_copy(half):
        return remote(
            w_cols.at[:, half], w_cols.at[:, half], d_ss.at[0], d_rs.at[0], (sibling, s)
        )

    def m_copy(to, b):
        return remote(
            m_own, m_all.at[b, pl.ds(0, ROWS)], m_ss.at[to], m_rs.at[b], (g, to)
        )

    def z_copy(to, slot):
        return remote(
            z_send.at[pl.ds(pl.multiple_of(to * FH, FH), FH)],
            z_recv.at[slot],
            z_ss.at[to],
            z_rs.at[slot],
            (g, to),
        )

    def p_copy(to, slot):
        return remote(o_ref, o_tiles.at[slot], p_ss.at[to], p_rs.at[slot], (g, to))

    def oy_copy(to, slot):
        return remote(
            o_all.at[y, core], o_all.at[slot, core], oy_ss.at[to], oy_rs.at[slot], (2 * to + core, s)
        )

    def od_copy(slot, half):
        return remote(
            o_all.at[slot, half], o_all.at[slot, half], od_ss.at[slot], od_rs.at[slot], (sibling, s)
        )

    def r_copy(to, slot):
        return remote(
            mixed_tr.at[pl.ds(pl.multiple_of(to * FH, FH), FH)],
            returned.at[slot],
            r_ss.at[to],
            r_rs.at[slot],
            (g, to),
        )

    barrier = pltpu.get_barrier_semaphore()

    def greet_sp(j):
        pl.semaphore_signal(barrier, inc=1, device_id=(g, sp_peer(j)), device_id_type=MESH)

    def greet_grp(j):
        pl.semaphore_signal(barrier, inc=1, device_id=(grp_peer(j), s), device_id_type=MESH)

    loop(1, N_SP, greet_sp)
    loop(1, N_GRP, greet_grp)

    embed = embed_ref[...].astype(F32)
    centered = embed - jnp.mean(embed, axis=1, keepdims=True)
    scaled = centered * scale_ref[...]
    scaled_hi = scaled.astype(BF16)
    shift = jnp.where(iota((16, D), 0) == 0, jnp.broadcast_to(shift_ref[...], (16, D)), 0.0)
    shift_hi = shift.astype(BF16)
    factors[pl.ds(0, 64), :] = scaled_hi
    factors[pl.ds(64, 16), :] = shift_hi
    factors[pl.ds(ROWS, 64), :] = (scaled - scaled_hi.astype(F32)).astype(BF16)
    factors[pl.ds(ROWS + 64, 16), :] = (shift - shift_hi.astype(F32)).astype(BF16)
    padded_embed[pl.ds(0, 64), :] = embed_ref[...]
    padded_embed[pl.ds(64, 64), :] = jnp.zeros((64, D), BF16)

    def fill_perm(j):
        base = pl.multiple_of(j * 64, 64)
        row = iota((64, TOKENS), 0) + base
        col = iota((64, TOKENS), 1)
        same = jnp.logical_and(
            jnp.right_shift(row, 5) == jnp.bitwise_and(col, 15),
            jnp.bitwise_and(row, 31) == jnp.right_shift(col, 4),
        )
        perm[pl.ds(base, 64), :] = one_hot(same)

    loop(0, TOKENS // 64, fill_perm)

    def pad_m(j):
        m_all[j, pl.ds(ROWS, 128 - ROWS), :] = jnp.zeros((128 - ROWS, 128), BF16)

    loop(0, BLOCKS, pad_m)

    pl.semaphore_wait(barrier, N_SP - 1 + N_GRP - 1)

    loop(1, N_GRP, lambda j: c_copy(grp_peer(j), g).start())
    c_recv[g] = coarse_ref[g]

    def send_w(j):
        b = lax.rem(j + block, BLOCKS)

        @pl.when(owner_of(b) != s)
        def _():
            w_copy(b, s).start()

    loop(0, BLOCKS, send_w)

    @pl.when(owner)
    def _():
        w_tiles[s] = w_ref[:, pl.ds(pl.multiple_of(block * 128, 128), 128)]

    def wait_c(j):
        c_copy(grp_peer(j), grp_peer(j)).wait_recv()

    loop(1, N_GRP, wait_c)
    lane = iota((FH, 128), 1)
    ones_lane = jnp.where(lane == 64, 1.0, 0.0)
    spread_row = iota((128, 512), 0)
    spread_col = iota((128, 512), 1)
    spread = one_hot(
        jnp.logical_and(
            jnp.right_shift(spread_row, 4) == jnp.right_shift(spread_col, 6),
            jnp.bitwise_and(spread_row, 15) == jnp.bitwise_and(spread_col, 15),
        )
    )
    for k in range(4):
        up = dot(c_recv[:, k, :].astype(BF16), spread)
        noise = noise_ref[:, k * 512 : (k + 1) * 512].astype(F32)
        mix = (signal_coef * up + noise_coef * noise).astype(BF16).astype(F32)
        for half in range(4):
            piece = mix[:, half * 128 : (half + 1) * 128]
            w = k * 8 + half * 2
            patches[w * FH : (w + 1) * FH, :] = jnp.where(lane < 64, piece, 0.0).astype(BF16)
            patches[(w + 1) * FH : (w + 2) * FH, :] = jnp.where(
                lane < 64, pltpu.roll(piece, 64, 1), 0.0
            ).astype(BF16)

    def norm_rows(j):
        rows = pl.ds(pl.multiple_of(j * 64, 64), 64)
        piece = patches[rows, :]
        h = dot(piece, padded_embed[...])
        mean = jnp.mean(h, axis=1, keepdims=True)
        away = h - mean
        var = jnp.mean(away * away, axis=1, keepdims=True)
        z = piece.astype(F32) * lax.rsqrt(var + epsilon)
        z_send[rows, :] = jnp.where(iota((64, 128), 1) == 64, 1.0, z).astype(BF16)

    loop(0, TOKENS // 64, norm_rows)
    loop(1, N_SP, lambda j: z_copy(sp_peer(j), s).start())
    z_recv[s] = z_send[pl.ds(pl.multiple_of(s * FH, FH), FH), :]

    @pl.when(owner)
    def _():
        def wait_w(j):
            w_copy(block, sp_peer(j)).wait_recv()

        loop(1, N_SP, wait_w)
        row = iota((PLANE_ROWS, 512), 0)
        col = iota((PLANE_ROWS, 512), 1)
        within = jnp.bitwise_and(col, 15)
        pick = one_hot(
            jnp.logical_and(within < 3, row == jnp.right_shift(col, 4) * 3 + within)
        )
        w_cols[y, core] = dot(pick, w_tiles[...].reshape(512, 128)).astype(BF16)
        loop(1, N_Y, lambda j: y_copy(y_peer(j), y).start())

    loop(1, N_SP, lambda j: p_copy(sp_peer(j), s).start())
    o_tiles[s] = o_ref[...]

    @pl.when(owner)
    def _():
        loop(1, N_Y, lambda j: y_copy(y_peer(j), y_peer(j)).wait_recv())
        d_copy(core).start()
        d_copy(1 - core).wait_recv()
        both = dot(factors[...], w_cols[...].reshape(D, 128))
        m_own[...] = (both[:ROWS] + both[ROWS:]).astype(BF16)
        loop(1, N_SP, lambda j: m_copy(sp_peer(j), block).start())
        m_all[block, pl.ds(0, ROWS), :] = m_own[...]

    loop(1, N_SP, lambda j: p_copy(sp_peer(j), sp_peer(j)).wait_recv())
    for j in range(HD // 128):
        row = iota((PLANE_ROWS, 1024), 0)
        col = iota((PLANE_ROWS, 1024), 1)
        within = jnp.bitwise_and(col, 31)
        first = jnp.right_shift(col, 5) * 3
        hit = jnp.logical_and(within == j, row == first)
        for i in (1, 2):
            hit = jnp.logical_or(
                hit, jnp.logical_and(within == 6 * i + j, row == first + i)
            )
        o_all[y, core, :, j * 128 : (j + 1) * 128] = dot(
            one_hot(hit), o_tiles[...].reshape(1024, 128)
        ).astype(BF16)
    loop(1, N_Y, lambda j: oy_copy(y_peer(j), y).start())
    od_copy(y, core).start()

    loop(1, N_SP, lambda j: z_copy(sp_peer(j), sp_peer(j)).wait_recv())

    def wait_m(b):
        @pl.when(owner_of(b) != s)
        def _():
            m_copy(owner_of(b), b).wait_recv()

    loop(0, BLOCKS, wait_m)
    z_rt = dot(perm[...], z_recv[...].reshape(TOKENS, 128)).astype(BF16)
    head_row = jnp.bitwise_and(iota((256, 128), 0), 127)
    head_col = iota((256, 128), 1)
    same_head = one_hot(
        jnp.right_shift(head_row, 6) == jnp.right_shift(head_col, 6)
    )
    ones_block = jnp.ones((128, 128), BF16)

    def clip_of(t):
        end = clip_ref[0, 0]
        clip = jnp.where(t >= end, 1, 0)
        for j in (1, 2, 3):
            end = end + clip_ref[0, j]
            clip = clip + jnp.where(t >= end, 1, 0)
        return clip

    mask_row = jnp.bitwise_and(iota((256, 128), 0), 127)
    mask_col = iota((256, 128), 1)
    allowed = jnp.logical_and(
        jnp.right_shift(mask_row, 5) == jnp.right_shift(mask_col, 5),
        clip_of(jnp.bitwise_and(mask_row, 31)) == clip_of(jnp.bitwise_and(mask_col, 31)),
    )
    low_half = iota((128, 128), 1) < 64

    def head_norm(flat, gains):
        squares = flat * flat
        hi = squares.astype(BF16)
        lo = (squares - hi.astype(F32)).astype(BF16)
        total = dot(jnp.concatenate([hi, lo], axis=1), same_head)
        return flat * lax.rsqrt(total * (1.0 / HEAD) + epsilon) * gains

    def pair(j):
        query = head_norm(dot(z_rt, m_all[j]), qg_ref[j]).astype(BF16)
        keys = head_norm(dot(z_rt, m_all[PAIRS + j]), kg_ref[j]).astype(BF16)
        values = dot(z_rt, m_all[2 * PAIRS + j]).astype(BF16)
        for tile in range(4):
            q = query[tile * 128 : (tile + 1) * 128]
            k = keys[tile * 128 : (tile + 1) * 128]
            v = values[tile * 128 : (tile + 1) * 128]
            zero = jnp.zeros_like(q)
            q_two = jnp.concatenate(
                [jnp.where(low_half, q, zero), jnp.where(low_half, zero, q)], axis=0
            )
            scores = jnp.where(allowed, dot_t(q_two, k) * (1.0 / 8.0), -1e30)
            top = jnp.max(scores, axis=1, keepdims=True)
            expo = jnp.exp(scores - top).astype(BF16)
            total = dot(expo, ones_block)
            both = dot(expo, v) / total
            mixed_rt[
                tile * 128 : (tile + 1) * 128, pl.ds(pl.multiple_of(j * 128, 128), 128)
            ] = jnp.where(low_half, both[:128], both[128:]).astype(BF16)

    loop(0, PAIRS, pair)
    for j in range(3):
        cols = slice(j * 256, (j + 1) * 256)
        mixed_tr[:, cols] = lax.dot_general(
            perm[...], mixed_rt[:, cols], (((0,), (0,)), ((), ())), preferred_element_type=F32
        ).astype(BF16)
    loop(1, N_SP, lambda j: r_copy(sp_peer(j), s).start())
    returned[s] = mixed_tr[pl.ds(pl.multiple_of(s * FH, FH), FH), :]

    natural = dot(perm[...], patches[...]).astype(BF16)
    for j in range(6):
        cols = slice(j * 256, (j + 1) * 256)
        hidden[:, cols] = dot(natural, padded_embed[:, cols]).astype(BF16)

    def pass_on(j):
        oy_copy(y_peer(j), y_peer(j)).wait_recv()
        od_copy(y_peer(j), core).start()

    loop(1, N_Y, pass_on)
    loop(1, N_SP, lambda j: r_copy(sp_peer(j), sp_peer(j)).wait_recv())
    loop(0, N_Y, lambda j: od_copy(j, 1 - core).wait_recv())

    for j in range(3):
        cols = slice(j * 256, (j + 1) * 256)
        mixed_rt[:, cols] = dot(perm[...], returned[:, :, cols].reshape(TOKENS, 256)).astype(BF16)
    for j in range(N_Y):
        cols = slice(j * 192, (j + 1) * 192)
        attn = dot_t(mixed_rt[...], o_all[j].reshape(192, HD))
        out_ref[:, cols] = (hidden[:, cols].astype(F32) + attn).astype(BF16)

    loop(1, N_GRP, lambda j: c_copy(grp_peer(j), g).wait_send())

    def end_w(b):
        @pl.when(owner_of(b) != s)
        def _():
            w_copy(b, s).wait_send()

    loop(0, BLOCKS, end_w)

    @pl.when(owner)
    def _():
        loop(1, N_Y, lambda j: y_copy(y_peer(j), y).wait_send())
        d_copy(core).wait_send()
        loop(1, N_SP, lambda j: m_copy(sp_peer(j), block).wait_send())

    loop(1, N_SP, lambda j: z_copy(sp_peer(j), s).wait_send())
    loop(1, N_SP, lambda j: p_copy(sp_peer(j), s).wait_send())
    loop(1, N_Y, lambda j: oy_copy(y_peer(j), y).wait_send())
    loop(0, N_Y, lambda j: od_copy(j, core).wait_send())
    loop(1, N_SP, lambda j: r_copy(sp_peer(j), s).wait_send())


def local(
    coarse_latent,
    renoise,
    clip_frames,
    patch_embed,
    mod_shift,
    mod_scale,
    qkv_weight,
    out_weight,
    q_gain,
    k_gain,
):
    coarse = coarse_latent.reshape(N_GRP, 4, 128).astype(F32)
    coarse = jnp.pad(coarse, ((0, 0), (0, 4), (0, 0)))
    w_rows = jnp.pad(qkv_weight, ((0, 13), (0, 0)))
    o_rows = jnp.pad(out_weight.reshape(18, 128), ((0, 14), (0, 0)))
    vmem = pl.BlockSpec(memory_space=pltpu.VMEM)
    smem = pl.BlockSpec(memory_space=pltpu.SMEM)
    dma = pltpu.SemaphoreType.DMA
    sizes = [16, 16, 32, 32, 8, 8, 1, 1, 32, 32, 32, 32, 32, 32, 8, 8, 8, 8, 32, 32]
    return pl.pallas_call(
        kernel,
        out_shape=jax.ShapeDtypeStruct((TOKENS, D), BF16),
        in_specs=[vmem, vmem, smem] + [vmem] * 7,
        out_specs=vmem,
        scratch_shapes=[
            pltpu.VMEM((N_GRP, 8, 128), F32),
            pltpu.VMEM((N_SP, 16, 128), BF16),
            pltpu.VMEM((N_Y, 2, PLANE_ROWS, 128), BF16),
            pltpu.VMEM((2 * ROWS, D), BF16),
            pltpu.VMEM((ROWS, 128), BF16),
            pltpu.VMEM((BLOCKS, 128, 128), BF16),
            pltpu.VMEM((TOKENS, 128), BF16),
            pltpu.VMEM((TOKENS, 128), BF16),
            pltpu.VMEM((N_SP, FH, 128), BF16),
            pltpu.VMEM((N_SP, 32, 128), BF16),
            pltpu.VMEM((N_Y, 2, PLANE_ROWS, HD), BF16),
            pltpu.VMEM((TOKENS, TOKENS), BF16),
            pltpu.VMEM((TOKENS, HD), BF16),
            pltpu.VMEM((TOKENS, HD), BF16),
            pltpu.VMEM((N_SP, FH, HD), BF16),
            pltpu.VMEM((128, D), BF16),
            pltpu.VMEM((TOKENS, D), BF16),
        ]
        + [dma((n,)) for n in sizes],
        compiler_params=pltpu.CompilerParams(
            collective_id=0, has_side_effects=True, vmem_limit_bytes=48 * 1024 * 1024
        ),
    )(
        coarse,
        renoise,
        clip_frames,
        patch_embed,
        mod_shift,
        mod_scale,
        w_rows,
        o_rows,
        q_gain.reshape(PAIRS, 1, 128),
        k_gain.reshape(PAIRS, 1, 128),
    )


def solution(mesh):
    placed = (
        P(None, "sp", "grp", None),
        P(("grp", "sp"), None),
        P("grp", None),
        P(),
        P("grp", None),
        P("grp", None),
        P(("grp", "sp"), None),
        P(("grp", "sp"), None),
        P(),
        P(),
    )
    return jax.shard_map(
        local, mesh=mesh, in_specs=placed, out_specs=P(("grp", "sp"), None), check_vma=False
    )
```

```python
import jax
import jax.numpy as jnp
from jax import lax
from jax.experimental import pallas as pl
from jax.experimental.pallas import tpu as pltpu
from jax.sharding import PartitionSpec as P

HEADS = 12
HEAD = 64
C = 16
FH = 16
FW = 32
D = 1536
HD = HEADS * HEAD
TOKENS = FH * FW
WINDOW = 16
N_GRP = 16
N_Y = 8
N_SP = 32
BLOCKS = 3 * HD // 128
PAIRS = HEADS // 2
ROWS = 80
PLANE_ROWS = 96

signal_coef = 0.8
noise_coef = 0.6
epsilon = 1e-06
MESH = pl.DeviceIdType.MESH
F32 = jnp.float32
BF16 = jnp.bfloat16


def iota(shape, axis):
    return lax.broadcasted_iota(jnp.int32, shape, axis)


def dot(a, b):
    return jnp.dot(a, b, preferred_element_type=F32)


def dot_t(a, b):
    return lax.dot_general(a, b, (((1,), (1,)), ((), ())), preferred_element_type=F32)


def one_hot(condition):
    return jnp.where(condition, 1.0, 0.0).astype(BF16)


def kernel(
    coarse_any,
    noise_any,
    clip_any,
    embed_any,
    shift_any,
    scale_any,
    w_any,
    o_any,
    qg_any,
    kg_any,
    out_ref,
    coarse_in,
    noise_ref,
    clip_ref,
    embed_ref,
    shift_ref,
    scale_ref,
    w_in,
    o_in,
    qg_ref,
    kg_ref,
    c_send,
    c_recv,
    w_ref,
    o_wide,
    o_ref,
    w_tiles,
    w_cols,
    factors,
    m_own,
    m_all,
    m_turned,
    patches,
    away_turned,
    z_all,
    z_wide,
    o_tiles,
    o_all,
    perm,
    query,
    dots,
    squares,
    probs,
    blended,
    mixed_turned,
    mixed,
    padded_embed,
    hidden,
    in_s,
    c_ss,
    c_rs,
    w_ss,
    w_rs,
    y_ss,
    y_rs,
    d_ss,
    d_rs,
    m_ss,
    m_rs,
    p_ss,
    p_rs,
    oy_ss,
    oy_rs,
    od_ss,
    od_rs,
    ax_ss,
    ax_rs,
    az_ss,
    az_rs,
    bz_ss,
    bz_rs,
    bx_ss,
    bx_rs,
):
    g = lax.axis_index("grp")
    s = lax.axis_index("sp")
    y = g // 2
    core = lax.rem(g, 2)
    sibling = g + 1 - 2 * core
    x = s // 8
    z = lax.rem(s, 8)
    block = (9 * s + 8) // 16
    owner = (16 * block) // 9 == s

    def sp_peer(j):
        return lax.rem(s + j, N_SP)

    def grp_peer(j):
        return lax.rem(g + j, N_GRP)

    def y_peer(j):
        return lax.rem(y + j, N_Y)

    def x_at(j):
        return lax.rem(x + j + 4, 4)

    def z_at(j):
        return lax.rem(z + j + 8, 8)

    def owner_of(b):
        return (16 * b) // 9

    def remote(src, dst, send_sem, recv_sem, to):
        return pltpu.make_async_remote_copy(
            src_ref=src,
            dst_ref=dst,
            send_sem=send_sem,
            recv_sem=recv_sem,
            device_id=to,
            device_id_type=MESH,
        )

    def loop(start, stop, body):
        def step(j, carry):
            body(j)
            return carry

        lax.fori_loop(start, stop, step, 0)

    def c_copy(to, slot):
        return remote(
            c_send.at[to], c_recv.at[slot], c_ss.at[to], c_rs.at[slot], (to, s)
        )

    def w_copy(b, slot):
        return remote(
            w_ref.at[:, pl.ds(pl.multiple_of(b * 128, 128), 128)],
            w_tiles.at[slot],
            w_ss.at[b],
            w_rs.at[slot],
            (g, owner_of(b)),
        )

    def y_copy(to, slot):
        return remote(
            w_cols.at[y, core], w_cols.at[slot, core], y_ss.at[to], y_rs.at[slot], (2 * to + core, s)
        )

    def d_copy(half):
        return remote(
            w_cols.at[:, half], w_cols.at[:, half], d_ss.at[0], d_rs.at[0], (sibling, s)
        )

    def m_copy(to, b):
        return remote(
            m_own, m_all.at[b, pl.ds(0, ROWS)], m_ss.at[to], m_rs.at[b], (g, to)
        )

    def p_copy(to, slot):
        return remote(o_ref, o_tiles.at[slot], p_ss.at[to], p_rs.at[slot], (g, to))

    def oy_copy(to, slot):
        return remote(
            o_all.at[y, core], o_all.at[slot, core], oy_ss.at[to], oy_rs.at[slot], (2 * to + core, s)
        )

    def od_copy(slot, half):
        return remote(
            o_all.at[slot, half], o_all.at[slot, half], od_ss.at[slot], od_rs.at[slot], (sibling, s)
        )

    def ax_copy(to, slot):
        part = z_all.at[slot, z, pl.ds(0, 32)]
        return remote(part, part, ax_ss.at[to], ax_rs.at[slot], (g, to * 8 + z))

    def az_copy(way, k, first):
        rows = (
            pl.ds(0, 4) if k < 3 else pl.ds(0, 2) if way == 0 else pl.ds(2, 2)
        )
        part = z_all.at[rows, z_at(first), pl.ds(0, 32)]
        to = z_at(1) if way == 0 else z_at(-1)
        return remote(part, part, az_ss.at[way, k], az_rs.at[way, k], (g, x * 8 + to))

    def bz_copy(way, k, first):
        rows = (
            pl.ds(32, 32) if k < 3 else pl.ds(32, 16) if way == 0 else pl.ds(48, 16)
        )
        part = z_all.at[x, z_at(first), rows]
        to = z_at(1) if way == 0 else z_at(-1)
        return remote(part, part, bz_ss.at[way, k], bz_rs.at[way, k], (g, x * 8 + to))

    def bx_copy(way, k, first):
        cols = pl.ds(0, 8) if k == 0 else pl.ds(0, 4) if way == 0 else pl.ds(4, 4)
        part = z_all.at[x_at(first), cols, pl.ds(32, 32)]
        to = x_at(1) if way == 0 else x_at(-1)
        return remote(part, part, bx_ss.at[way, k], bx_rs.at[way, k], (g, to * 8 + z))

    def ring_send(copy, k):
        copy(0, k, -k).start()
        copy(1, k, k).start()

    def ring_wait(copy, k):
        copy(0, k, -1 - k).wait_recv()
        copy(1, k, 1 + k).wait_recv()

    def ring_end(copy, k):
        copy(0, k, -k).wait_send()
        copy(1, k, k).wait_send()

    pairs = [
        (w_any, w_in),
        (coarse_any, coarse_in),
        (o_any, o_in),
        (noise_any, noise_ref),
        (embed_any, embed_ref),
        (scale_any, scale_ref),
        (shift_any, shift_ref),
        (clip_any, clip_ref),
        (qg_any, qg_ref),
        (kg_any, kg_ref),
    ]
    loads = [pltpu.make_async_copy(a, b, in_s.at[i]) for i, (a, b) in enumerate(pairs)]
    for load in loads:
        load.start()

    barrier = pltpu.get_barrier_semaphore()

    def greet_sp(j):
        pl.semaphore_signal(barrier, inc=1, device_id=(g, sp_peer(j)), device_id_type=MESH)

    def greet_grp(j):
        pl.semaphore_signal(barrier, inc=1, device_id=(grp_peer(j), s), device_id_type=MESH)

    loop(1, N_SP, greet_sp)
    loop(1, N_GRP, greet_grp)

    w_ref[...] = jnp.zeros((16, 3 * HD), BF16)
    o_wide[...] = jnp.zeros((32, 128), F32)
    for load in loads[:3]:
        load.wait()
    w_ref[0:3, :] = w_in[...]
    coarse = coarse_in[...].reshape(N_GRP, FW * C).astype(F32)
    for k in range(4):
        c_send[:, k, :] = coarse[:, k * 128 : (k + 1) * 128]
    o_rows = o_in[...].astype(F32)
    for j in range(6):
        o_wide[4 * j : 4 * j + 3, :] = o_rows[:, j * 128 : (j + 1) * 128]
    o_ref[...] = o_wide[...].astype(BF16)

    pl.semaphore_wait(barrier, N_SP - 1 + N_GRP - 1)

    loop(1, N_GRP, lambda j: c_copy(grp_peer(j), g).start())
    c_recv[g] = c_send[g]

    def send_w(j):
        b = lax.rem(j + block, BLOCKS)

        @pl.when(owner_of(b) != s)
        def _():
            w_copy(b, s).start()

    loop(0, BLOCKS, send_w)

    @pl.when(owner)
    def _():
        w_tiles[s] = w_ref[:, pl.ds(pl.multiple_of(block * 128, 128), 128)]

    loop(1, N_SP, lambda j: p_copy(sp_peer(j), s).start())
    o_tiles[s] = o_ref[...]

    for load in loads[3:]:
        load.wait()
    embed = embed_ref[...].astype(F32)
    centered = embed - jnp.mean(embed, axis=1, keepdims=True)
    away_hi = centered.astype(BF16).astype(F32)
    away = jnp.concatenate([away_hi, (centered - away_hi).astype(BF16).astype(F32)], axis=0)
    away_turned[...] = away.T.astype(BF16)
    scaled = centered * scale_ref[...]
    scaled_hi = scaled.astype(BF16)
    shift = jnp.where(iota((16, D), 0) == 0, jnp.broadcast_to(shift_ref[...], (16, D)), 0.0)
    shift_hi = shift.astype(BF16)
    factors[pl.ds(0, 64), :] = scaled_hi
    factors[pl.ds(64, 16), :] = shift_hi
    factors[pl.ds(ROWS, 64), :] = (scaled - scaled_hi.astype(F32)).astype(BF16)
    factors[pl.ds(ROWS + 64, 16), :] = (shift - shift_hi.astype(F32)).astype(BF16)
    padded_embed[pl.ds(0, 64), :] = embed_ref[...]
    padded_embed[pl.ds(64, 64), :] = jnp.zeros((64, D), BF16)
    gains = qg_ref[...] * kg_ref[...] * (1.0 / 8.0)
    gains_turned = jnp.broadcast_to(gains.reshape(1, HD), (128, HD)).T

    def fill_perm(j):
        base = pl.multiple_of(j * 64, 64)
        row = iota((64, TOKENS), 0) + base
        col = iota((64, TOKENS), 1)
        same = jnp.logical_and(
            jnp.right_shift(row, 5) == jnp.bitwise_and(col, 15),
            jnp.bitwise_and(row, 31) == jnp.right_shift(col, 4),
        )
        perm[pl.ds(base, 64), :] = one_hot(same)

    loop(0, TOKENS // 64, fill_perm)

    def pad_m(j):
        m_all[j, pl.ds(ROWS, 128 - ROWS), :] = jnp.zeros((128 - ROWS, 128), BF16)

    loop(0, BLOCKS, pad_m)
    ones_row = one_hot(iota((16, TOKENS), 0) == 0)

    def pad_z(j):
        z_all[j // 8, lax.rem(j, 8), pl.ds(64, 16), :] = ones_row

    loop(0, N_SP, pad_z)

    def pad_blended(j):
        blended[j, pl.ds(64, 16), :] = ones_row

    loop(0, HEADS, pad_blended)

    lane = iota((FH, 128), 1)
    spread_row = iota((128, 512), 0)
    spread_col = iota((128, 512), 1)
    spread = one_hot(
        jnp.logical_and(
            jnp.right_shift(spread_row, 4) == jnp.right_shift(spread_col, 6),
            jnp.bitwise_and(spread_row, 15) == jnp.bitwise_and(spread_col, 15),
        )
    )
    eye = one_hot(iota((128, 128), 0) == iota((128, 128), 1))
    twice = one_hot(jnp.bitwise_and(iota((128, 128), 0), 63) == iota((128, 128), 1))

    def wait_c(j):
        c_copy(grp_peer(j), grp_peer(j)).wait_recv()

    loop(1, N_GRP, wait_c)
    for k in range(4):
        up = dot(c_recv[:, k, :].astype(BF16), spread)
        noise = noise_ref[:, k * 512 : (k + 1) * 512].astype(F32)
        mix = (signal_coef * up + noise_coef * noise).astype(BF16).astype(F32)
        for half in range(4):
            piece = mix[:, half * 128 : (half + 1) * 128]
            w = k * 8 + half * 2
            patches[w * FH : (w + 1) * FH, :] = jnp.where(lane < 64, piece, 0.0).astype(BF16)
            patches[(w + 1) * FH : (w + 2) * FH, :] = jnp.where(
                lane < 64, pltpu.roll(piece, 64, 1), 0.0
            ).astype(BF16)
    turned = dot_t(twice, patches[...])
    turned_two = turned.astype(BF16)
    total = jnp.zeros((1, TOKENS), F32)
    for j in range(6):
        part = dot(away_turned[j * 256 : (j + 1) * 256, :], turned_two)
        total = total + jnp.sum(part * part, axis=0, keepdims=True)
    inverse = lax.rsqrt(total * (1.0 / D) + epsilon)
    z_all[x, z, pl.ds(0, 64), :] = (turned[:64] * inverse).astype(BF16)
    for j in (1, 3, 2):
        ax_copy(x_at(j), x).start()
    ring_send(bz_copy, 0)

    @pl.when(owner)
    def _():
        def wait_w(j):
            w_copy(block, sp_peer(j)).wait_recv()

        loop(1, N_SP, wait_w)
        row = iota((PLANE_ROWS, 512), 0)
        col = iota((PLANE_ROWS, 512), 1)
        within = jnp.bitwise_and(col, 15)
        pick = one_hot(
            jnp.logical_and(within < 3, row == jnp.right_shift(col, 4) * 3 + within)
        )
        w_cols[y, core] = dot(pick, w_tiles[...].reshape(512, 128)).astype(BF16)
        loop(1, N_Y, lambda j: y_copy(y_peer(j), y).start())

    ring_wait(bz_copy, 0)
    ring_send(bz_copy, 1)
    for j in (1, 3, 2):
        ax_copy(x, x_at(j)).wait_recv()
    ring_send(az_copy, 0)

    loop(1, N_SP, lambda j: p_copy(sp_peer(j), sp_peer(j)).wait_recv())
    row = iota((PLANE_ROWS, 1024), 0)
    col = iota((PLANE_ROWS, 1024), 1)
    within = jnp.bitwise_and(col, 31)
    third = jnp.bitwise_and(within, 3)
    fits = jnp.logical_and(third < 3, row == jnp.right_shift(col, 5) * 3 + third)
    for j in range(HD // 128):
        pick = one_hot(jnp.logical_and(fits, jnp.right_shift(within, 2) == j))
        o_all[y, core, :, j * 128 : (j + 1) * 128] = dot(
            pick, o_tiles[...].reshape(1024, 128)
        ).astype(BF16)
    loop(1, N_Y, lambda j: oy_copy(y_peer(j), y).start())
    od_copy(y, core).start()

    ring_wait(bz_copy, 1)
    ring_send(bz_copy, 2)
    ring_wait(az_copy, 0)
    ring_send(az_copy, 1)
    ring_wait(bz_copy, 2)
    ring_send(bz_copy, 3)

    @pl.when(owner)
    def _():
        loop(1, N_Y, lambda j: y_copy(y_peer(j), y_peer(j)).wait_recv())
        d_copy(core).start()
        d_copy(1 - core).wait_recv()
        both = dot(factors[...], w_cols[...].reshape(D, 128))
        m_own[...] = (both[:ROWS] + both[ROWS:]).astype(BF16)
        loop(1, N_SP, lambda j: m_copy(sp_peer(j), block).start())
        m_all[block, pl.ds(0, ROWS), :] = m_own[...]

    ring_wait(bz_copy, 3)
    ring_send(bx_copy, 0)
    ring_wait(az_copy, 1)
    ring_send(az_copy, 2)

    natural = dot(perm[...], patches[...]).astype(BF16)
    for j in range(6):
        cols = slice(j * 256, (j + 1) * 256)
        hidden[:, cols] = dot(natural, padded_embed[:, cols]).astype(BF16)

    ring_wait(az_copy, 2)
    ring_send(az_copy, 3)
    ring_wait(bx_copy, 0)
    bx_copy(0, 1, -1).start()
    bx_copy(1, 1, 1).start()

    def wait_m(b):
        @pl.when(owner_of(b) != s)
        def _():
            m_copy(owner_of(b), b).wait_recv()

        m_turned[pl.ds(pl.multiple_of(b * 128, 128), 128), :] = dot_t(eye, m_all[b])[
            :, :ROWS
        ].astype(BF16)

    loop(0, BLOCKS, wait_m)
    own = z_all[x, z]
    for j in range(PAIRS):
        rows = slice(j * 128, (j + 1) * 128)
        q = dot(m_turned[rows, :], own).reshape(2, HEAD, TOKENS)
        level = jnp.sum(q * q, axis=1, keepdims=True) * (1.0 / HEAD) + epsilon
        q = (q * lax.rsqrt(level)).reshape(128, TOKENS)
        gain = jnp.concatenate([gains_turned[rows]] * 4, axis=1)
        query[rows, :] = q * gain

    def pass_on(j):
        oy_copy(y_peer(j), y_peer(j)).wait_recv()
        od_copy(y_peer(j), core).start()

    loop(1, N_Y, pass_on)

    ring_wait(az_copy, 3)
    bx_copy(0, 1, -2).wait_recv()
    bx_copy(1, 1, 2).wait_recv()

    ends = [clip_ref[0, 0]]
    for j in (1, 2, 3):
        ends.append(ends[-1] + clip_ref[0, j])
    first = jnp.int32(0)
    last = ends[0]
    for j in (1, 2, 3):
        inside = s >= ends[j - 1]
        first = jnp.where(inside, ends[j - 1], first)
        last = jnp.where(inside, ends[j], last)
    base = jnp.minimum(first, N_SP - WINDOW)

    def frame(j):
        t = base + j
        entries = z_all[jnp.right_shift(t, 3), jnp.bitwise_and(t, 7)]
        z_wide[j] = entries[:64].astype(F32)
        for pair in range(PAIRS):
            rows = slice(pair * 128, (pair + 1) * 128)
            k = dot(m_turned[HD + pair * 128 : HD + (pair + 1) * 128, :], entries)
            dots[j, pl.ds(2 * pair, 2), :] = jnp.sum(
                (k * query[rows, :]).reshape(2, HEAD, TOKENS), axis=1
            )
            squares[j, pl.ds(2 * pair, 2), :] = jnp.sum(
                (k * k).reshape(2, HEAD, TOKENS), axis=1
            )

    loop(0, WINDOW, frame)
    order = iota((WINDOW, HEADS, TOKENS), 0) + base
    valid = jnp.logical_and(order >= first, order < last)
    scores = dots[...] * lax.rsqrt(squares[...] * (1.0 / HEAD) + epsilon)
    scores = jnp.where(valid, scores, -1e30)
    expo = jnp.exp(scores - jnp.max(scores, axis=0, keepdims=True))
    probs[...] = expo / jnp.sum(expo, axis=0, keepdims=True)

    def head(h):
        total = jnp.zeros((HEAD, TOKENS), F32)
        for j in range(WINDOW):
            total = total + probs[j, pl.ds(h, 1), :] * z_wide[j]
        blended[h, pl.ds(0, 64), :] = total.astype(BF16)
        rows = pl.ds(pl.multiple_of(h * HEAD, HEAD), HEAD)
        value_rows = pl.ds(pl.multiple_of(2 * HD + h * HEAD, HEAD), HEAD)
        mixed_turned[rows, :] = dot(m_turned[value_rows, :], blended[h]).astype(BF16)

    loop(0, HEADS, head)

    loop(0, N_Y, lambda j: od_copy(j, 1 - core).wait_recv())
    for j in range(3):
        cols = slice(j * 256, (j + 1) * 256)
        mixed[:, cols] = dot_t(perm[...], mixed_turned[cols, :]).astype(BF16)
    for j in range(N_Y):
        cols = slice(j * 192, (j + 1) * 192)
        attn = dot_t(mixed[...], o_all[j].reshape(192, HD))
        out_ref[:, cols] = (hidden[:, cols].astype(F32) + attn).astype(BF16)

    loop(1, N_GRP, lambda j: c_copy(grp_peer(j), g).wait_send())

    def end_w(b):
        @pl.when(owner_of(b) != s)
        def _():
            w_copy(b, s).wait_send()

    loop(0, BLOCKS, end_w)

    @pl.when(owner)
    def _():
        loop(1, N_Y, lambda j: y_copy(y_peer(j), y).wait_send())
        d_copy(core).wait_send()
        loop(1, N_SP, lambda j: m_copy(sp_peer(j), block).wait_send())

    loop(1, N_SP, lambda j: p_copy(sp_peer(j), s).wait_send())
    loop(1, N_Y, lambda j: oy_copy(y_peer(j), y).wait_send())
    loop(0, N_Y, lambda j: od_copy(j, core).wait_send())
    for j in (1, 3, 2):
        ax_copy(x_at(j), x).wait_send()
    for k in range(4):
        ring_end(az_copy, k)
        ring_end(bz_copy, k)
    ring_end(bx_copy, 0)
    bx_copy(0, 1, -1).wait_send()
    bx_copy(1, 1, 1).wait_send()


def local(
    coarse_latent,
    renoise,
    clip_frames,
    patch_embed,
    mod_shift,
    mod_scale,
    qkv_weight,
    out_weight,
    q_gain,
    k_gain,
):
    dma = pltpu.SemaphoreType.DMA
    sems = [10, 16, 16, 32, 32, 8, 8, 1, 1, 32, 32, 32, 32, 8, 8, 8, 8, 4, 4]
    rings = [(2, 4)] * 4 + [(2, 2)] * 2
    args = (
        coarse_latent,
        renoise,
        clip_frames,
        patch_embed,
        mod_shift,
        mod_scale,
        qkv_weight,
        out_weight,
        q_gain,
        k_gain,
    )
    inputs = [
        (pltpu.SMEM if a.dtype == jnp.int32 else pltpu.VMEM)(a.shape, a.dtype) for a in args
    ]
    return pl.pallas_call(
        kernel,
        out_shape=jax.ShapeDtypeStruct((TOKENS, D), BF16),
        in_specs=[pl.BlockSpec(memory_space=pl.ANY)] * len(args),
        out_specs=pl.BlockSpec(memory_space=pltpu.VMEM),
        scratch_shapes=inputs
        + [
            pltpu.VMEM((N_GRP, 8, 128), F32),
            pltpu.VMEM((N_GRP, 8, 128), F32),
            pltpu.VMEM((16, 3 * HD), BF16),
            pltpu.VMEM((32, 128), F32),
            pltpu.VMEM((32, 128), BF16),
            pltpu.VMEM((N_SP, 16, 128), BF16),
            pltpu.VMEM((N_Y, 2, PLANE_ROWS, 128), BF16),
            pltpu.VMEM((2 * ROWS, D), BF16),
            pltpu.VMEM((ROWS, 128), BF16),
            pltpu.VMEM((BLOCKS, 128, 128), BF16),
            pltpu.VMEM((3 * HD, ROWS), BF16),
            pltpu.VMEM((TOKENS, 128), BF16),
            pltpu.VMEM((D, 128), BF16),
            pltpu.VMEM((4, 8, ROWS, TOKENS), BF16),
            pltpu.VMEM((WINDOW, HEAD, TOKENS), F32),
            pltpu.VMEM((N_SP, 32, 128), BF16),
            pltpu.VMEM((N_Y, 2, PLANE_ROWS, HD), BF16),
            pltpu.VMEM((TOKENS, TOKENS), BF16),
            pltpu.VMEM((HD, TOKENS), F32),
            pltpu.VMEM((WINDOW, HEADS, TOKENS), F32),
            pltpu.VMEM((WINDOW, HEADS, TOKENS), F32),
            pltpu.VMEM((WINDOW, HEADS, TOKENS), F32),
            pltpu.VMEM((HEADS, ROWS, TOKENS), BF16),
            pltpu.VMEM((HD, TOKENS), BF16),
            pltpu.VMEM((TOKENS, HD), BF16),
            pltpu.VMEM((128, D), BF16),
            pltpu.VMEM((TOKENS, D), BF16),
        ]
        + [dma((n,)) for n in sems]
        + [dma(n) for n in rings],
        compiler_params=pltpu.CompilerParams(
            collective_id=0, has_side_effects=True, vmem_limit_bytes=48 * 1024 * 1024
        ),
    )(*args)


def solution(mesh):
    placed = (
        P(None, "sp", "grp", None),
        P(("grp", "sp"), None),
        P("grp", None),
        P(),
        P("grp", None),
        P("grp", None),
        P(("grp", "sp"), None),
        P(("grp", "sp"), None),
        P(),
        P(),
    )
    return jax.shard_map(
        local, mesh=mesh, in_specs=placed, out_specs=P(("grp", "sp"), None), check_vma=False
    )
```

```python
import jax
import jax.numpy as jnp
from jax import lax
from jax.experimental import pallas as pl
from jax.experimental.pallas import tpu as pltpu
from jax.sharding import PartitionSpec as P

HEADS = 12
HEAD = 64
C = 16
FH = 16
FW = 32
D = 1536
HD = HEADS * HEAD
TOKENS = FH * FW
WINDOW = 16
N_GRP = 16
N_Y = 8
N_SP = 32
BLOCKS = 3 * HD // 128
PAIRS = HEADS // 2
ROWS = 80
PLANE_ROWS = 96

signal_coef = 0.8
noise_coef = 0.6
epsilon = 1e-06
MESH = pl.DeviceIdType.MESH
F32 = jnp.float32
BF16 = jnp.bfloat16


def iota(shape, axis):
    return lax.broadcasted_iota(jnp.int32, shape, axis)


def dot(a, b):
    return jnp.dot(a, b, preferred_element_type=F32)


def dot_t(a, b):
    return lax.dot_general(a, b, (((1,), (1,)), ((), ())), preferred_element_type=F32)


def one_hot(condition):
    return jnp.where(condition, 1.0, 0.0).astype(BF16)


def kernel(
    coarse_any,
    noise_any,
    clip_any,
    embed_any,
    shift_any,
    scale_any,
    w_any,
    o_any,
    qg_any,
    kg_any,
    out_ref,
    coarse_in,
    noise_ref,
    clip_ref,
    embed_ref,
    shift_ref,
    scale_ref,
    w_in,
    o_in,
    qg_ref,
    kg_ref,
    c_send,
    c_recv,
    w_ref,
    o_wide,
    o_ref,
    w_tiles,
    w_cols,
    sibling_scale,
    sibling_shift,
    factors,
    m_own,
    m_all,
    m_turned,
    patches,
    noise_rows,
    coarse_rows,
    cov,
    n_near,
    n_far,
    k_near,
    k_far,
    z_wide,
    o_tiles,
    o_own,
    o_bands,
    o_all,
    perm,
    query,
    keys_a,
    keys_b,
    dots,
    squares,
    probs,
    blended,
    mixed_turned,
    mixed,
    padded_embed,
    hidden,
    in_s,
    c_ss,
    c_rs,
    w_ss,
    w_rs,
    y_ss,
    y_rs,
    d_ss,
    d_rs,
    m_ss,
    m_rs,
    pz_ss,
    pz_rs,
    px_ss,
    px_rs,
    od_ss,
    od_rs,
    kz_ss,
    kz_rs,
    kx_ss,
    kx_rs,
    o2_ss,
    o2_rs,
    n2_ss,
    n2_rs,
    nr_ss,
    nr_rs,
    nx_ss,
    nx_rs,
):
    g = lax.axis_index("grp")
    s = lax.axis_index("sp")
    y = g // 2
    core = lax.rem(g, 2)
    sibling = g + 1 - 2 * core
    x = s // 8
    z = lax.rem(s, 8)
    half = z // 4
    place = x * 4 + lax.rem(z, 4)
    first_pick = lax.rem(place, 2) == core
    owner = jnp.logical_or(first_pick, jnp.logical_or(place == 12, place == 13))
    block = jnp.where(first_pick, place, place + 4)
    plane = core * N_SP + s

    def sp_peer(j):
        return lax.rem(s + j, N_SP)

    def grp_peer(j):
        return lax.rem(g + j, N_GRP)

    def y_peer(j):
        return lax.rem(y + j, N_Y)

    def x_at(j):
        return lax.rem(x + j + 4, 4)

    def z_at(j):
        return lax.rem(z + j + 8, 8)

    def owner_core(b):
        return jnp.where(b < 16, lax.rem(b, 2), 1 - lax.rem(b, 2))

    def owner_sp(b, part):
        q = jnp.where(b < 16, b, b - 4)
        return (q // 4) * 8 + part * 4 + lax.rem(q, 4)

    def not_here(b, part):
        return jnp.logical_or(owner_core(b) != core, owner_sp(b, part) != s)

    def remote(src, dst, send_sem, recv_sem, to):
        return pltpu.make_async_remote_copy(
            src_ref=src,
            dst_ref=dst,
            send_sem=send_sem,
            recv_sem=recv_sem,
            device_id=to,
            device_id_type=MESH,
        )

    def loop(start, stop, body):
        def step(j, carry):
            body(j)
            return carry

        lax.fori_loop(start, stop, step, 0)

    def c_copy(to, slot):
        return remote(
            c_send.at[to], c_recv.at[slot], c_ss.at[to], c_rs.at[slot], (to, s)
        )

    def w_copy(b, part, slot):
        return remote(
            w_ref.at[:, pl.ds(pl.multiple_of(b * 128, 128), 128)],
            w_tiles.at[slot],
            w_ss.at[2 * b + part],
            w_rs.at[slot],
            (2 * y + owner_core(b), owner_sp(b, part)),
        )

    def y_copy(to, slot):
        return remote(
            w_cols.at[y], w_cols.at[slot], y_ss.at[to], y_rs.at[slot], (2 * to + core, s)
        )

    def d_copies():
        to = (sibling, s)
        return [
            remote(scale_ref, sibling_scale, d_ss.at[0], d_rs.at[0], to),
            remote(shift_ref, sibling_shift, d_ss.at[1], d_rs.at[1], to),
        ]

    def m_target(i):
        return i // 16, (lax.rem(i, 16) // 4) * 8 + half * 4 + lax.rem(i, 4)

    def m_copy(i, b):
        at_core, at_sp = m_target(i)
        return remote(
            m_own.at[at_core],
            m_all.at[b, pl.ds(0, ROWS)],
            m_ss.at[i],
            m_rs.at[b],
            (2 * y + at_core, at_sp),
        )

    def pz_copy(to, slot):
        return remote(o_ref, o_tiles.at[slot], pz_ss.at[to], pz_rs.at[slot], (g, x * 8 + to))

    def px_copy(to, slot):
        return remote(o_own, o_bands.at[slot], px_ss.at[to], px_rs.at[slot], (g, to * 8 + z))

    def od_copy(slot, half):
        return remote(
            o_all.at[slot, half], o_all.at[slot, half], od_ss.at[slot], od_rs.at[slot], (sibling, s)
        )

    def kz_copy(to, slot):
        part = k_near.at[1, slot]
        return remote(part, part, kz_ss.at[to], kz_rs.at[slot], (g, x * 8 + to))

    def kx_copy(way, k):
        if k == 0:
            src, dst = k_near.at[1], k_near.at[2 * way]
        else:
            half_row = pl.ds(4 * way, 4)
            src, dst = k_near.at[2 * way, half_row], k_far.at[half_row]
        to = x_at(1) if way == 0 else x_at(-1)
        return remote(src, dst, kx_ss.at[way, k], kx_rs.at[way, k], (g, to * 8 + z))

    moves = [(1, 0, 0), (-1, 0, 0), (2, 0, 0), (-2, 0, 0), (1, -2, 0), (-1, 2, 0), (2, -2, 1), (-2, 2, 2)]

    def ring_copy(view, at, to, sems, i, start):
        part = view(at(start), moves[i][2])
        return remote(part, part, sems[0].at[i], sems[1].at[i], to(at(moves[i][0])))

    def ring_send(ring, i):
        ring_copy(*ring, i, moves[i][1]).start()

    def ring_wait(ring, i):
        ring_copy(*ring, i, moves[i][1] - moves[i][0]).wait_recv()

    def ring_end(ring, i):
        ring_copy(*ring, i, moves[i][1]).wait_send()

    def o_view(slot, part):
        rows = (pl.ds(0, PLANE_ROWS), pl.ds(0, 48), pl.ds(48, 48))[part]
        return o_all.at[slot, core, rows]

    def n_view(slot, part):
        rows = (pl.ds(0, 64), pl.ds(0, 32), pl.ds(32, 32))[part]
        return n_near.at[1, slot, rows]

    def y_at(j):
        return lax.rem(y + j + N_Y, N_Y)

    o_ring = (o_view, y_at, lambda to: (2 * to + core, s), (o2_ss, o2_rs))
    n_ring = (n_view, z_at, lambda to: (g, x * 8 + to), (n2_ss, n2_rs))

    offsets = [0, -1, 1, -2, 2, -3, 3, -4]

    def nx_copy(way, i):
        slot = z_at(offsets[i])
        to = x_at(1) if way == 0 else x_at(-1)
        return remote(
            n_near.at[1, slot],
            n_near.at[2 * way, slot],
            nx_ss.at[way, i],
            nx_rs.at[way, i],
            (g, to * 8 + z),
        )

    def nr_copy(i):
        slot = z_at(offsets[i])
        way = i % 2
        to = x_at(1) if way == 0 else x_at(-1)
        return remote(
            n_near.at[2 * way, slot], n_far.at[slot], nr_ss.at[i], nr_rs.at[i], (g, to * 8 + z)
        )

    def spread_frames(indices):
        for i in indices:
            nx_copy(0, i).start()
            nx_copy(1, i).start()

    def relay_frames(indices):
        for i in indices:
            nx_copy(0, i).wait_recv()
            nx_copy(1, i).wait_recv()
            nr_copy(i).start()

    pairs = [
        (w_any, w_in),
        (coarse_any, coarse_in),
        (o_any, o_in),
        (noise_any, noise_ref),
        (scale_any, scale_ref),
        (shift_any, shift_ref),
        (embed_any, embed_ref),
        (clip_any, clip_ref),
        (qg_any, qg_ref),
        (kg_any, kg_ref),
    ]
    loads = [pltpu.make_async_copy(a, b, in_s.at[i]) for i, (a, b) in enumerate(pairs)]
    for load in loads:
        load.start()

    barrier = pltpu.get_barrier_semaphore()

    def greet_plane(j):
        other = lax.rem(plane + j, 2 * N_SP)
        pl.semaphore_signal(
            barrier,
            inc=1,
            device_id=(2 * y + other // N_SP, lax.rem(other, N_SP)),
            device_id_type=MESH,
        )

    def greet_y(j):
        for c in (0, 1):
            pl.semaphore_signal(
                barrier, inc=1, device_id=(2 * y_peer(j) + c, s), device_id_type=MESH
            )

    loop(1, 2 * N_SP, greet_plane)
    loop(1, N_Y, greet_y)

    w_ref[...] = jnp.zeros((16, 3 * HD), BF16)
    o_wide[...] = jnp.zeros((32, 128), F32)
    for load in loads[:6]:
        load.wait()
    w_ref[0:3, :] = w_in[...]
    coarse = coarse_in[...].astype(F32)
    for k in range(4):
        c_send[:, k, :] = coarse[:, k * 128 : (k + 1) * 128]
    o_rows = o_in[...].astype(F32)
    for j in range(6):
        o_wide[4 * j : 4 * j + 3, :] = o_rows[:, j * 128 : (j + 1) * 128]
    o_ref[...] = o_wide[...].astype(BF16)

    lane = iota((FH, 128), 1)
    eye = one_hot(iota((128, 128), 0) == iota((128, 128), 1))

    def to_positions(ref, k, piece):
        ref[2 * k * FH : (2 * k + 1) * FH, :] = jnp.where(lane < 64, piece, 0.0).astype(BF16)
        ref[(2 * k + 1) * FH : (2 * k + 2) * FH, :] = jnp.where(
            lane < 64, pltpu.roll(piece, 64, 1), 0.0
        ).astype(BF16)

    for k in range(16):
        to_positions(noise_rows, k, noise_ref[:, k * 128 : (k + 1) * 128].astype(F32))
    n_near[1, z] = dot_t(eye[:64], noise_rows[...]).astype(BF16)

    pl.semaphore_wait(barrier, 2 * N_SP - 1 + 2 * (N_Y - 1))

    loop(1, N_GRP, lambda j: c_copy(grp_peer(j), g).start())
    c_recv[g] = c_send[g]
    for copy in d_copies():
        copy.start()

    def send_w(j):
        m = lax.rem(j + 4 * place, 2 * BLOCKS)
        b = m // 2
        part = lax.rem(m, 2)

        @pl.when(not_here(b, part))
        def _():
            w_copy(b, part, plane).start()

    loop(0, 2 * BLOCKS, send_w)

    @pl.when(owner)
    def _():
        w_tiles[plane] = w_ref[:, pl.ds(pl.multiple_of(block * 128, 128), 128)]

    for j in (4, 3, 5, 2, 6, 1, 7):
        pz_copy(z_at(j), z).start()
    o_tiles[z] = o_ref[...]

    for load in loads[6:]:
        load.wait()
    embed = embed_ref[...].astype(F32)
    centered = embed - jnp.mean(embed, axis=1, keepdims=True)
    away_hi = centered.astype(BF16)
    away = jnp.concatenate([away_hi, (centered - away_hi.astype(F32)).astype(BF16)], axis=0)
    gram = dot_t(away, away) * (1.0 / D)
    gram = gram[:64] + gram[64:]
    gram = (gram + pltpu.roll(gram, 64, 1))[:, :64]
    for j in range(3):
        part = gram.astype(BF16)
        cov[j * 64 : (j + 1) * 64, :] = part
        gram = gram - part.astype(F32)

    def set_factors(at, scale, shift):
        scaled = centered * scale
        scaled_hi = scaled.astype(BF16)
        shift = jnp.where(iota((16, D), 0) == 0, jnp.broadcast_to(shift, (16, D)), 0.0)
        shift_hi = shift.astype(BF16)
        factors[at, pl.ds(0, 64), :] = scaled_hi
        factors[at, pl.ds(64, 16), :] = shift_hi
        factors[at, pl.ds(ROWS, 64), :] = (scaled - scaled_hi.astype(F32)).astype(BF16)
        factors[at, pl.ds(ROWS + 64, 16), :] = (shift - shift_hi.astype(F32)).astype(BF16)

    for copy in d_copies():
        copy.wait_recv()

    @pl.when(owner)
    def _():
        set_factors(core, scale_ref[...], shift_ref[...])
        set_factors(1 - core, sibling_scale[...], sibling_shift[...])

    padded_embed[pl.ds(0, 64), :] = embed_ref[...]
    padded_embed[pl.ds(64, 64), :] = jnp.zeros((64, D), BF16)
    gains = qg_ref[...] * kg_ref[...] * (1.0 / 8.0)
    gains_turned = jnp.broadcast_to(gains.reshape(1, HD), (128, HD)).T

    def fill_perm(j):
        base = pl.multiple_of(j * 64, 64)
        row = iota((64, TOKENS), 0) + base
        col = iota((64, TOKENS), 1)
        same = jnp.logical_and(
            jnp.right_shift(row, 5) == jnp.bitwise_and(col, 15),
            jnp.bitwise_and(row, 31) == jnp.right_shift(col, 4),
        )
        perm[pl.ds(base, 64), :] = one_hot(same)

    loop(0, TOKENS // 64, fill_perm)

    def pad_m(j):
        m_all[j, pl.ds(ROWS, 128 - ROWS), :] = jnp.zeros((128 - ROWS, 128), BF16)

    loop(0, BLOCKS, pad_m)
    ones_row = one_hot(iota((16, TOKENS), 0) == 0)

    def pad_blended(j):
        blended[j, pl.ds(64, 16), :] = ones_row

    loop(0, HEADS, pad_blended)

    for i in range(4):
        ring_send(n_ring, i)
    spread_frames([0])

    @pl.when(owner)
    def _():
        def wait_w(j):
            w_copy(block, half, lax.rem(plane + j, 2 * N_SP)).wait_recv()

        loop(1, 2 * N_SP, wait_w)
        row = iota((2 * PLANE_ROWS, 1024), 0)
        col = iota((2 * PLANE_ROWS, 1024), 1)
        within = jnp.bitwise_and(col, 15)
        pick = one_hot(
            jnp.logical_and(within < 3, row == jnp.right_shift(col, 4) * 3 + within)
        )
        w_cols[y] = dot(pick, w_tiles[...].reshape(1024, 128)).astype(BF16)
        loop(1, N_Y, lambda j: y_copy(y_peer(j), y).start())

    for j in (1, 7, 2, 6, 3, 5, 4):
        pz_copy(z, z_at(j)).wait_recv()
    row = iota((144, 256), 0)
    col = iota((144, 256), 1)
    third = jnp.bitwise_and(col, 3)
    column = jnp.right_shift(jnp.bitwise_and(col, 31), 2)
    pick_rows = one_hot(
        jnp.logical_and(third < 3, row == column * 24 + jnp.right_shift(col, 5) * 3 + third)
    )
    o_own[...] = dot(pick_rows, o_tiles[...].reshape(256, 128)).astype(BF16)
    for j in (2, 1, 3):
        px_copy(x_at(j), x).start()
    o_bands[x] = o_own[...]

    spread_row = iota((128, 512), 0)
    spread_col = iota((128, 512), 1)
    spread = one_hot(
        jnp.logical_and(
            jnp.right_shift(spread_row, 4) == jnp.right_shift(spread_col, 6),
            jnp.bitwise_and(spread_row, 15) == jnp.bitwise_and(spread_col, 15),
        )
    )

    def wait_c(j):
        c_copy(grp_peer(j), grp_peer(j)).wait_recv()

    loop(1, N_GRP, wait_c)
    for k in range(4):
        up = dot(c_recv[:, k, :].astype(BF16), spread)
        for j in range(4):
            to_positions(coarse_rows, k * 4 + j, up[:, j * 128 : (j + 1) * 128])
    k_near[1, z] = dot_t(eye[:16], coarse_rows[...]).astype(BF16)
    for j in (4, 3, 5, 2, 6, 1, 7):
        kz_copy(z_at(j), z).start()

    for i in (0, 1):
        ring_wait(n_ring, i)
    spread_frames([1, 2])
    for i in (2, 3):
        ring_wait(n_ring, i)
    for i in (4, 5, 6, 7):
        ring_send(n_ring, i)
    spread_frames([3, 4])

    relay_frames([0])
    patches[...] = (
        signal_coef * coarse_rows[...].astype(F32) + noise_coef * noise_rows[...].astype(F32)
    ).astype(BF16)

    for j in (1, 3, 2):
        px_copy(x, x_at(j)).wait_recv()
    bands = [o_bands[j].astype(F32) for j in range(4)]
    for j in range(HD // 128):
        o_all[y, core, :, j * 128 : (j + 1) * 128] = jnp.concatenate(
            [band[j * 24 : (j + 1) * 24] for band in bands], axis=0
        ).astype(BF16)
    for i in range(4):
        ring_send(o_ring, i)
    od_copy(y, core).start()

    for i in (4, 5, 6, 7):
        ring_wait(n_ring, i)
    spread_frames([5, 6, 7])
    for j in (1, 7, 2, 6, 3, 5, 4):
        kz_copy(z, z_at(j)).wait_recv()
    kx_copy(0, 0).start()
    kx_copy(1, 0).start()
    relay_frames([1, 2, 3, 4])

    @pl.when(owner)
    def _():
        loop(1, N_Y, lambda j: y_copy(y_peer(j), y_peer(j)).wait_recv())
        cols = w_cols[...].reshape(D, 128)
        for c in (0, 1):
            both = dot(factors[c], cols)
            m_own[c] = (both[:ROWS] + both[ROWS:]).astype(BF16)

        def send_m(i):
            at_core, at_sp = m_target(i)

            @pl.when(jnp.logical_or(at_core != core, at_sp != s))
            def _():
                m_copy(i, block).start()

        loop(0, 2 * FH, send_m)
        m_all[block, pl.ds(0, ROWS), :] = m_own[core]

    relay_frames([5, 6, 7])

    kx_copy(0, 0).wait_recv()
    kx_copy(1, 0).wait_recv()
    kx_copy(0, 1).start()
    kx_copy(1, 1).start()

    natural = dot(perm[...], patches[...]).astype(BF16)
    for j in range(6):
        cols = slice(j * 256, (j + 1) * 256)
        hidden[:, cols] = dot(natural, padded_embed[:, cols]).astype(BF16)

    for i in range(4):
        ring_wait(o_ring, i)
    for i in (4, 5, 6, 7):
        ring_send(o_ring, i)
    for j in (1, -1, 2, -2):
        od_copy(y_at(j), core).start()

    def wait_m(b):
        @pl.when(not_here(b, half))
        def _():
            m_copy(core * 16 + place, b).wait_recv()

    def turn_m(blocks):
        for b in blocks:
            m_turned[b * 128 : (b + 1) * 128, :] = dot_t(eye, m_all[b])[:, :ROWS].astype(BF16)

    def frame_entries(coarse, noise):
        coarse = coarse.astype(F32)
        noise = noise.astype(F32)
        up = jnp.concatenate([coarse] * 4, axis=0)
        patch = (signal_coef * up + noise_coef * noise).astype(BF16)
        wide = patch.astype(F32)
        turned = dot(cov[...], patch)
        var = jnp.sum(wide * (turned[:64] + turned[64:128] + turned[128:]), axis=0, keepdims=True)
        wide = wide * lax.rsqrt(jnp.maximum(var, 0.0) + epsilon)
        return wide, jnp.concatenate([wide.astype(BF16), ones_row], axis=0)

    loop(0, 2 * PAIRS, wait_m)
    turn_m(range(2 * PAIRS))
    own = frame_entries(k_near[1, z], n_near[1, z])[1]
    for j in range(PAIRS):
        rows = slice(j * 128, (j + 1) * 128)
        q = dot(m_turned[rows, :], own).reshape(2, HEAD, TOKENS)
        level = jnp.sum(q * q, axis=1, keepdims=True) * (1.0 / HEAD) + epsilon
        q = (q * lax.rsqrt(level)).reshape(128, TOKENS)
        gain = jnp.concatenate([gains_turned[rows]] * 4, axis=1)
        query[rows, :] = q * gain

    ends = [clip_ref[0, 0]]
    for j in (1, 2, 3):
        ends.append(ends[-1] + clip_ref[0, j])
    first = jnp.int32(0)
    last = ends[0]
    for j in (1, 2, 3):
        inside = s >= ends[j - 1]
        first = jnp.where(inside, ends[j - 1], first)
        last = jnp.where(inside, ends[j], last)
    base = jnp.minimum(first, N_SP - WINDOW)

    near = jnp.minimum(jnp.maximum(s - base - WINDOW // 4, 0), WINDOW // 2)

    def frame_at(j):
        return base + jnp.bitwise_and(near + j, WINDOW - 1)

    def keys_of(j, buffer, far):
        t = frame_at(j)
        at_z = jnp.bitwise_and(t, 7)
        row = jnp.right_shift(t, 3) - x + 1
        near_row = jnp.minimum(jnp.maximum(row, 0), 2)
        coarse = k_near[near_row, at_z]
        noise = n_near[near_row, at_z]
        if far:
            inside = row == near_row
            coarse = jnp.where(inside, coarse, k_far[at_z])
            noise = jnp.where(inside, noise, n_far[at_z])
        wide, entries = frame_entries(coarse, noise)
        z_wide[j] = wide
        buffer[...] = dot(m_turned[HD : 2 * HD, :], entries)

    def score(j, buffer):
        for h in range(HEADS):
            k = buffer[h * HEAD : (h + 1) * HEAD, :]
            q = query[h * HEAD : (h + 1) * HEAD, :]
            dots[j, h] = jnp.sum((k * q).reshape(8, 8, TOKENS), axis=0)
            squares[j, h] = jnp.sum((k * k).reshape(8, 8, TOKENS), axis=0)

    def two_frames(far):
        def body(j):
            keys_of(2 * j + 1, keys_b, far)
            score(2 * j, keys_a)
            keys_of(after(2 * j + 2), keys_a, far)
            score(2 * j + 1, keys_b)

        return body

    def after(j):
        return jnp.where(j == WINDOW // 2, j - 1, jnp.minimum(j, WINDOW - 1))

    keys_of(0, keys_a, False)
    loop(0, WINDOW // 4, two_frames(False))
    kx_copy(0, 1).wait_recv()
    kx_copy(1, 1).wait_recv()
    for i in range(8):
        nr_copy(i).wait_recv()
    keys_of(WINDOW // 2, keys_a, True)
    loop(WINDOW // 4, WINDOW // 2, two_frames(True))
    for i in (4, 5, 6, 7):
        ring_wait(o_ring, i)
    for j in (3, -3, 4):
        od_copy(y_at(j), core).start()
    loop(2 * PAIRS, BLOCKS, wait_m)
    turn_m(range(2 * PAIRS, BLOCKS))
    def reduce_frame(j):
        scale = lax.rsqrt(jnp.sum(squares[j], axis=1) * (1.0 / HEAD) + epsilon)
        t = frame_at(j)
        valid = jnp.logical_and(t >= first, t < last)
        probs[j] = jnp.where(valid, jnp.sum(dots[j], axis=1) * scale, -1e30)

    loop(0, WINDOW, reduce_frame)
    expo = jnp.exp(probs[...] - jnp.max(probs[...], axis=0, keepdims=True))
    probs[...] = expo / jnp.sum(expo, axis=0, keepdims=True)

    def head(h):
        total = jnp.zeros((HEAD, TOKENS), F32)
        for j in range(WINDOW):
            total = total + probs[j, pl.ds(h, 1), :] * z_wide[j]
        blended[h, pl.ds(0, 64), :] = total.astype(BF16)

    loop(0, HEADS, head)
    for h in range(HEADS):
        rows = slice(h * HEAD, (h + 1) * HEAD)
        mixed_turned[rows, :] = dot(
            m_turned[2 * HD + h * HEAD : 2 * HD + (h + 1) * HEAD, :], blended[h]
        ).astype(BF16)

    loop(0, N_Y, lambda j: od_copy(j, 1 - core).wait_recv())
    for j in range(3):
        cols = slice(j * 256, (j + 1) * 256)
        mixed[:, cols] = dot_t(perm[...], mixed_turned[cols, :]).astype(BF16)
    for j in range(N_Y):
        cols = slice(j * 192, (j + 1) * 192)
        attn = dot_t(mixed[...], o_all[j].reshape(192, HD))
        out_ref[:, cols] = (hidden[:, cols].astype(F32) + attn).astype(BF16)

    loop(1, N_GRP, lambda j: c_copy(grp_peer(j), g).wait_send())

    def end_w(m):
        b = m // 2
        part = lax.rem(m, 2)

        @pl.when(not_here(b, part))
        def _():
            w_copy(b, part, plane).wait_send()

    loop(0, 2 * BLOCKS, end_w)
    for copy in d_copies():
        copy.wait_send()

    @pl.when(owner)
    def _():
        loop(1, N_Y, lambda j: y_copy(y_peer(j), y).wait_send())

        def end_m(i):
            at_core, at_sp = m_target(i)

            @pl.when(jnp.logical_or(at_core != core, at_sp != s))
            def _():
                m_copy(i, block).wait_send()

        loop(0, 2 * FH, end_m)

    for j in range(1, 8):
        pz_copy(z_at(j), z).wait_send()
    for j in (1, 2, 3):
        px_copy(x_at(j), x).wait_send()
    loop(0, N_Y, lambda j: od_copy(j, core).wait_send())
    for i in range(8):
        ring_end(n_ring, i)
        ring_end(o_ring, i)
        nx_copy(0, i).wait_send()
        nx_copy(1, i).wait_send()
        nr_copy(i).wait_send()
    for j in range(1, 8):
        kz_copy(z_at(j), z).wait_send()
    kx_copy(0, 0).wait_send()
    kx_copy(1, 0).wait_send()
    kx_copy(0, 1).wait_send()
    kx_copy(1, 1).wait_send()


def local(
    coarse_latent,
    renoise,
    clip_frames,
    patch_embed,
    mod_shift,
    mod_scale,
    qkv_weight,
    out_weight,
    q_gain,
    k_gain,
):
    dma = pltpu.SemaphoreType.DMA
    sems = [10, 16, 16, 36, 64, 8, 8, 2, 2, 32, 18, 8, 8, 4, 4, 8, 8, 8, 8] + [(2, 2)] * 2 + [8] * 6
    rings = [(2, 8)] * 2
    args = (
        coarse_latent.transpose(1, 2, 0, 3).reshape(N_GRP, FW * C),
        renoise,
        clip_frames,
        patch_embed,
        mod_shift,
        mod_scale,
        qkv_weight,
        out_weight,
        q_gain,
        k_gain,
    )
    inputs = [
        (pltpu.SMEM if a.dtype == jnp.int32 else pltpu.VMEM)(a.shape, a.dtype) for a in args
    ]
    return pl.pallas_call(
        kernel,
        out_shape=jax.ShapeDtypeStruct((TOKENS, D), BF16),
        in_specs=[pl.BlockSpec(memory_space=pltpu.HBM)] * len(args),
        out_specs=pl.BlockSpec(memory_space=pltpu.VMEM),
        scratch_shapes=inputs
        + [
            pltpu.VMEM((N_GRP, 8, 128), F32),
            pltpu.VMEM((N_GRP, 8, 128), F32),
            pltpu.VMEM((16, 3 * HD), BF16),
            pltpu.VMEM((32, 128), F32),
            pltpu.VMEM((32, 128), BF16),
            pltpu.VMEM((2 * N_SP, 16, 128), BF16),
            pltpu.VMEM((N_Y, 2 * PLANE_ROWS, 128), BF16),
            pltpu.VMEM((1, D), F32),
            pltpu.VMEM((1, D), F32),
            pltpu.VMEM((2, 2 * ROWS, D), BF16),
            pltpu.VMEM((2, ROWS, 128), BF16),
            pltpu.VMEM((BLOCKS, 128, 128), BF16),
            pltpu.VMEM((3 * HD, ROWS), BF16),
            pltpu.VMEM((TOKENS, 128), BF16),
            pltpu.VMEM((TOKENS, 128), BF16),
            pltpu.VMEM((TOKENS, 128), BF16),
            pltpu.VMEM((192, 64), BF16),
            pltpu.VMEM((3, 8, 64, TOKENS), BF16),
            pltpu.VMEM((8, 64, TOKENS), BF16),
            pltpu.VMEM((3, 8, 16, TOKENS), BF16),
            pltpu.VMEM((8, 16, TOKENS), BF16),
            pltpu.VMEM((WINDOW, HEAD, TOKENS), F32),
            pltpu.VMEM((8, 32, 128), BF16),
            pltpu.VMEM((144, 128), BF16),
            pltpu.VMEM((4, 144, 128), BF16),
            pltpu.VMEM((N_Y, 2, PLANE_ROWS, HD), BF16),
            pltpu.VMEM((TOKENS, TOKENS), BF16),
            pltpu.VMEM((HD, TOKENS), F32),
            pltpu.VMEM((HD, TOKENS), F32),
            pltpu.VMEM((HD, TOKENS), F32),
            pltpu.VMEM((WINDOW, HEADS, 8, TOKENS), F32),
            pltpu.VMEM((WINDOW, HEADS, 8, TOKENS), F32),
            pltpu.VMEM((WINDOW, HEADS, TOKENS), F32),
            pltpu.VMEM((HEADS, ROWS, TOKENS), BF16),
            pltpu.VMEM((HD, TOKENS), BF16),
            pltpu.VMEM((TOKENS, HD), BF16),
            pltpu.VMEM((128, D), BF16),
            pltpu.VMEM((TOKENS, D), BF16),
        ]
        + [dma(n if isinstance(n, tuple) else (n,)) for n in sems]
        + [dma(n) for n in rings],
        compiler_params=pltpu.CompilerParams(
            collective_id=0, has_side_effects=True, vmem_limit_bytes=63 * 1024 * 1024
        ),
    )(*args)


def solution(mesh):
    placed = (
        P(None, "sp", "grp", None),
        P(("grp", "sp"), None),
        P("grp", None),
        P(),
        P("grp", None),
        P("grp", None),
        P(("grp", "sp"), None),
        P(("grp", "sp"), None),
        P(),
        P(),
    )
    return jax.shard_map(
        local, mesh=mesh, in_specs=placed, out_specs=P(("grp", "sp"), None), check_vma=False
    )
```

```python
import jax
import jax.numpy as jnp
from jax import lax
from jax.experimental import pallas as pl
from jax.experimental.pallas import tpu as pltpu
from jax.sharding import PartitionSpec as P

HEADS = 12
HEAD = 64
C = 16
FH = 16
FW = 32
D = 1536
HD = HEADS * HEAD
TOKENS = FH * FW
WINDOW = 16
N_GRP = 16
N_Y = 8
N_SP = 32
BLOCKS = 3 * HD // 128
PAIRS = HEADS // 2
ROWS = 80
PLANE_ROWS = 96

signal_coef = 0.8
noise_coef = 0.6
epsilon = 1e-06
MESH = pl.DeviceIdType.MESH
F32 = jnp.float32
BF16 = jnp.bfloat16


def iota(shape, axis):
    return lax.broadcasted_iota(jnp.int32, shape, axis)


def dot(a, b):
    return jnp.dot(a, b, preferred_element_type=F32)


def dot_t(a, b):
    return lax.dot_general(a, b, (((1,), (1,)), ((), ())), preferred_element_type=F32)


def one_hot(condition):
    return jnp.where(condition, 1.0, 0.0).astype(BF16)


def kernel(
    coarse_any,
    noise_any,
    clip_any,
    embed_any,
    shift_any,
    scale_any,
    w_any,
    o_any,
    qg_any,
    kg_any,
    out_ref,
    coarse_in,
    noise_ref,
    clip_ref,
    embed_ref,
    shift_ref,
    scale_ref,
    w_in,
    o_in,
    qg_ref,
    kg_ref,
    c_send,
    c_recv,
    w_ref,
    o_wide,
    o_ref,
    w_tiles,
    w_cols,
    sibling_scale,
    sibling_shift,
    factors,
    m_own,
    m_all,
    m_turned,
    patches,
    noise_rows,
    coarse_rows,
    cov,
    n_near,
    n_far,
    k_near,
    k_far,
    z_wide,
    o_tiles,
    o_own,
    o_bands,
    o_all,
    perm,
    query,
    keys_a,
    keys_b,
    dots,
    squares,
    probs,
    blended,
    mixed_turned,
    mixed,
    padded_embed,
    hidden,
    result,
    in_s,
    out_s,
    c_ss,
    c_rs,
    w_ss,
    w_rs,
    y_ss,
    y_rs,
    d_ss,
    d_rs,
    m_ss,
    m_rs,
    pz_ss,
    pz_rs,
    px_ss,
    px_rs,
    od_ss,
    od_rs,
    kz_ss,
    kz_rs,
    kx_ss,
    kx_rs,
    o2_ss,
    o2_rs,
    n2_ss,
    n2_rs,
    nr_ss,
    nr_rs,
    nx_ss,
    nx_rs,
):
    g = lax.axis_index("grp")
    s = lax.axis_index("sp")
    y = g // 2
    core = lax.rem(g, 2)
    sibling = g + 1 - 2 * core
    x = s // 8
    z = lax.rem(s, 8)
    half = z // 4
    place = x * 4 + lax.rem(z, 4)
    first_pick = lax.rem(place, 2) == core
    owner = jnp.logical_or(first_pick, jnp.logical_or(place == 12, place == 13))
    block = jnp.where(first_pick, place, place + 4)
    plane = core * N_SP + s

    def sp_peer(j):
        return lax.rem(s + j, N_SP)

    def grp_peer(j):
        return lax.rem(g + j, N_GRP)

    def y_peer(j):
        return lax.rem(y + j, N_Y)

    def x_at(j):
        return lax.rem(x + j + 4, 4)

    def z_at(j):
        return lax.rem(z + j + 8, 8)

    def owner_core(b):
        return jnp.where(b < 16, lax.rem(b, 2), 1 - lax.rem(b, 2))

    def owner_sp(b, part):
        q = jnp.where(b < 16, b, b - 4)
        return (q // 4) * 8 + part * 4 + lax.rem(q, 4)

    def not_here(b, part):
        return jnp.logical_or(owner_core(b) != core, owner_sp(b, part) != s)

    def remote(src, dst, send_sem, recv_sem, to):
        return pltpu.make_async_remote_copy(
            src_ref=src,
            dst_ref=dst,
            send_sem=send_sem,
            recv_sem=recv_sem,
            device_id=to,
            device_id_type=MESH,
        )

    def loop(start, stop, body):
        def step(j, carry):
            body(j)
            return carry

        lax.fori_loop(start, stop, step, 0)

    def c_copy(to, slot):
        return remote(
            c_send.at[to], c_recv.at[slot], c_ss.at[to], c_rs.at[slot], (to, s)
        )

    def w_copy(b, part, slot):
        return remote(
            w_ref.at[:, pl.ds(pl.multiple_of(b * 128, 128), 128)],
            w_tiles.at[slot],
            w_ss.at[2 * b + part],
            w_rs.at[slot],
            (2 * y + owner_core(b), owner_sp(b, part)),
        )

    def y_copy(to, slot):
        return remote(
            w_cols.at[y], w_cols.at[slot], y_ss.at[to], y_rs.at[slot], (2 * to + core, s)
        )

    def d_copies():
        to = (sibling, s)
        return [
            remote(scale_ref, sibling_scale, d_ss.at[0], d_rs.at[0], to),
            remote(shift_ref, sibling_shift, d_ss.at[1], d_rs.at[1], to),
        ]

    def m_target(i):
        return i // 16, (lax.rem(i, 16) // 4) * 8 + half * 4 + lax.rem(i, 4)

    def m_copy(i, b):
        at_core, at_sp = m_target(i)
        return remote(
            m_own.at[at_core],
            m_all.at[b, pl.ds(0, ROWS)],
            m_ss.at[i],
            m_rs.at[b],
            (2 * y + at_core, at_sp),
        )

    def pz_copy(to, slot):
        return remote(o_ref, o_tiles.at[slot], pz_ss.at[to], pz_rs.at[slot], (g, x * 8 + to))

    def px_copy(to, slot):
        return remote(o_own, o_bands.at[slot], px_ss.at[to], px_rs.at[slot], (g, to * 8 + z))

    def od_copy(slot, half):
        return remote(
            o_all.at[slot, half], o_all.at[slot, half], od_ss.at[slot], od_rs.at[slot], (sibling, s)
        )

    def kz_copy(to, slot):
        part = k_near.at[1, slot]
        return remote(part, part, kz_ss.at[to], kz_rs.at[slot], (g, x * 8 + to))

    def kx_copy(way, k):
        if k == 0:
            src, dst = k_near.at[1], k_near.at[2 * way]
        else:
            half_row = pl.ds(4 * way, 4)
            src, dst = k_near.at[2 * way, half_row], k_far.at[half_row]
        to = x_at(1) if way == 0 else x_at(-1)
        return remote(src, dst, kx_ss.at[way, k], kx_rs.at[way, k], (g, to * 8 + z))

    moves = [(1, 0, 0), (-1, 0, 0), (2, 0, 0), (-2, 0, 0), (1, -2, 0), (-1, 2, 0), (2, -2, 1), (-2, 2, 2)]

    def ring_copy(view, at, to, sems, i, start):
        part = view(at(start), moves[i][2])
        return remote(part, part, sems[0].at[i], sems[1].at[i], to(at(moves[i][0])))

    def ring_send(ring, i):
        ring_copy(*ring, i, moves[i][1]).start()

    def ring_wait(ring, i):
        ring_copy(*ring, i, moves[i][1] - moves[i][0]).wait_recv()

    def ring_end(ring, i):
        ring_copy(*ring, i, moves[i][1]).wait_send()

    def o_view(slot, part):
        rows = (pl.ds(0, PLANE_ROWS), pl.ds(0, 48), pl.ds(48, 48))[part]
        return o_all.at[slot, core, rows]

    def n_view(slot, part):
        rows = (pl.ds(0, 64), pl.ds(0, 32), pl.ds(32, 32))[part]
        return n_near.at[1, slot, rows]

    def y_at(j):
        return lax.rem(y + j + N_Y, N_Y)

    o_ring = (o_view, y_at, lambda to: (2 * to + core, s), (o2_ss, o2_rs))
    n_ring = (n_view, z_at, lambda to: (g, x * 8 + to), (n2_ss, n2_rs))

    offsets = [0, -1, 1, -2, 2, -3, 3, -4]

    def nx_copy(way, i):
        slot = z_at(offsets[i])
        to = x_at(1) if way == 0 else x_at(-1)
        return remote(
            n_near.at[1, slot],
            n_near.at[2 * way, slot],
            nx_ss.at[way, i],
            nx_rs.at[way, i],
            (g, to * 8 + z),
        )

    def nr_copy(i):
        slot = z_at(offsets[i])
        way = i % 2
        to = x_at(1) if way == 0 else x_at(-1)
        return remote(
            n_near.at[2 * way, slot], n_far.at[slot], nr_ss.at[i], nr_rs.at[i], (g, to * 8 + z)
        )

    def spread_frames(indices):
        for i in indices:
            nx_copy(0, i).start()
            nx_copy(1, i).start()

    def relay_frames(indices):
        for i in indices:
            nx_copy(0, i).wait_recv()
            nx_copy(1, i).wait_recv()
            nr_copy(i).start()

    pairs = [
        (w_any, w_in),
        (coarse_any, coarse_in),
        (o_any, o_in),
        (noise_any, noise_ref),
        (scale_any, scale_ref),
        (shift_any, shift_ref),
        (embed_any, embed_ref),
        (clip_any, clip_ref),
        (qg_any, qg_ref),
        (kg_any, kg_ref),
    ]
    loads = [pltpu.make_async_copy(a, b, in_s.at[i]) for i, (a, b) in enumerate(pairs)]
    for load in loads:
        load.start()

    barrier = pltpu.get_barrier_semaphore()

    def greet_plane(j):
        other = lax.rem(plane + j, 2 * N_SP)
        pl.semaphore_signal(
            barrier,
            inc=1,
            device_id=(2 * y + other // N_SP, lax.rem(other, N_SP)),
            device_id_type=MESH,
        )

    def greet_y(j):
        for c in (0, 1):
            pl.semaphore_signal(
                barrier, inc=1, device_id=(2 * y_peer(j) + c, s), device_id_type=MESH
            )

    loop(1, 2 * N_SP, greet_plane)
    loop(1, N_Y, greet_y)

    w_ref[...] = jnp.zeros((16, 3 * HD), BF16)
    o_wide[...] = jnp.zeros((32, 128), F32)
    for load in loads[:6]:
        load.wait()
    w_ref[0:3, :] = w_in[...]
    coarse = coarse_in[...].astype(F32)
    for k in range(4):
        c_send[:, k, :] = coarse[:, k * 128 : (k + 1) * 128]
    o_rows = o_in[...].astype(F32)
    for j in range(6):
        o_wide[4 * j : 4 * j + 3, :] = o_rows[:, j * 128 : (j + 1) * 128]
    o_ref[...] = o_wide[...].astype(BF16)

    lane = iota((FH, 128), 1)
    eye = one_hot(iota((128, 128), 0) == iota((128, 128), 1))

    def to_positions(ref, k, piece):
        ref[2 * k * FH : (2 * k + 1) * FH, :] = jnp.where(lane < 64, piece, 0.0).astype(BF16)
        ref[(2 * k + 1) * FH : (2 * k + 2) * FH, :] = jnp.where(
            lane < 64, pltpu.roll(piece, 64, 1), 0.0
        ).astype(BF16)

    for k in range(16):
        to_positions(noise_rows, k, noise_ref[:, k * 128 : (k + 1) * 128].astype(F32))
    n_near[1, z] = dot_t(eye[:64], noise_rows[...]).astype(BF16)

    pl.semaphore_wait(barrier, 2 * N_SP - 1 + 2 * (N_Y - 1))

    loop(1, N_GRP, lambda j: c_copy(grp_peer(j), g).start())
    c_recv[g] = c_send[g]
    for copy in d_copies():
        copy.start()

    def send_w(j):
        m = lax.rem(j + 4 * place, 2 * BLOCKS)
        b = m // 2
        part = lax.rem(m, 2)

        @pl.when(not_here(b, part))
        def _():
            w_copy(b, part, plane).start()

    for i in range(4):
        ring_send(n_ring, i)
    spread_frames([0])
    loop(0, 2 * BLOCKS, send_w)

    @pl.when(owner)
    def _():
        w_tiles[plane] = w_ref[:, pl.ds(pl.multiple_of(block * 128, 128), 128)]

    for j in (4, 3, 5, 2, 6, 1, 7):
        pz_copy(z_at(j), z).start()
    o_tiles[z] = o_ref[...]

    for load in loads[6:]:
        load.wait()
    embed = embed_ref[...].astype(F32)
    centered = embed - jnp.mean(embed, axis=1, keepdims=True)
    away_hi = centered.astype(BF16)
    away = jnp.concatenate([away_hi, (centered - away_hi.astype(F32)).astype(BF16)], axis=0)
    gram = dot_t(away, away) * (1.0 / D)
    gram = gram[:64] + gram[64:]
    gram = (gram + pltpu.roll(gram, 64, 1))[:, :64]
    for j in range(3):
        part = gram.astype(BF16)
        cov[j * 64 : (j + 1) * 64, :] = part
        gram = gram - part.astype(F32)

    def set_factors(at, scale, shift):
        scaled = centered * scale
        scaled_hi = scaled.astype(BF16)
        shift = jnp.where(iota((16, D), 0) == 0, jnp.broadcast_to(shift, (16, D)), 0.0)
        shift_hi = shift.astype(BF16)
        factors[at, pl.ds(0, 64), :] = scaled_hi
        factors[at, pl.ds(64, 16), :] = shift_hi
        factors[at, pl.ds(ROWS, 64), :] = (scaled - scaled_hi.astype(F32)).astype(BF16)
        factors[at, pl.ds(ROWS + 64, 16), :] = (shift - shift_hi.astype(F32)).astype(BF16)

    for copy in d_copies():
        copy.wait_recv()

    @pl.when(owner)
    def _():
        set_factors(core, scale_ref[...], shift_ref[...])
        set_factors(1 - core, sibling_scale[...], sibling_shift[...])

    padded_embed[pl.ds(0, 64), :] = embed_ref[...]
    padded_embed[pl.ds(64, 64), :] = jnp.zeros((64, D), BF16)
    gains = qg_ref[...] * kg_ref[...] * (1.0 / 8.0)
    gains_turned = jnp.broadcast_to(gains.reshape(1, HD), (128, HD)).T

    def fill_perm(j):
        base = pl.multiple_of(j * 64, 64)
        row = iota((64, TOKENS), 0) + base
        col = iota((64, TOKENS), 1)
        same = jnp.logical_and(
            jnp.right_shift(row, 5) == jnp.bitwise_and(col, 15),
            jnp.bitwise_and(row, 31) == jnp.right_shift(col, 4),
        )
        perm[pl.ds(base, 64), :] = one_hot(same)

    loop(0, TOKENS // 64, fill_perm)

    def pad_m(j):
        m_all[j, pl.ds(ROWS, 128 - ROWS), :] = jnp.zeros((128 - ROWS, 128), BF16)

    loop(0, BLOCKS, pad_m)
    ones_row = one_hot(iota((16, TOKENS), 0) == 0)

    def pad_blended(j):
        blended[j, pl.ds(64, 16), :] = ones_row

    loop(0, HEADS, pad_blended)


    for i in (0, 1):
        ring_wait(n_ring, i)
    spread_frames([1, 2])
    for i in (2, 3):
        ring_wait(n_ring, i)
    for i in (4, 5, 6, 7):
        ring_send(n_ring, i)
    spread_frames([3, 4])

    @pl.when(owner)
    def _():
        def wait_w(j):
            w_copy(block, half, lax.rem(plane + j, 2 * N_SP)).wait_recv()

        loop(1, 2 * N_SP, wait_w)
        row = iota((2 * PLANE_ROWS, 1024), 0)
        col = iota((2 * PLANE_ROWS, 1024), 1)
        within = jnp.bitwise_and(col, 15)
        pick = one_hot(
            jnp.logical_and(within < 3, row == jnp.right_shift(col, 4) * 3 + within)
        )
        w_cols[y] = dot(pick, w_tiles[...].reshape(1024, 128)).astype(BF16)
        loop(1, N_Y, lambda j: y_copy(y_peer(j), y).start())

    for j in (1, 7, 2, 6, 3, 5, 4):
        pz_copy(z, z_at(j)).wait_recv()
    row = iota((144, 256), 0)
    col = iota((144, 256), 1)
    third = jnp.bitwise_and(col, 3)
    column = jnp.right_shift(jnp.bitwise_and(col, 31), 2)
    pick_rows = one_hot(
        jnp.logical_and(third < 3, row == column * 24 + jnp.right_shift(col, 5) * 3 + third)
    )
    o_own[...] = dot(pick_rows, o_tiles[...].reshape(256, 128)).astype(BF16)
    for j in (2, 1, 3):
        px_copy(x_at(j), x).start()
    o_bands[x] = o_own[...]

    spread_row = iota((128, 512), 0)
    spread_col = iota((128, 512), 1)
    spread = one_hot(
        jnp.logical_and(
            jnp.right_shift(spread_row, 4) == jnp.right_shift(spread_col, 6),
            jnp.bitwise_and(spread_row, 15) == jnp.bitwise_and(spread_col, 15),
        )
    )

    def wait_c(j):
        c_copy(grp_peer(j), grp_peer(j)).wait_recv()

    loop(1, N_GRP, wait_c)
    for k in range(4):
        up = dot(c_recv[:, k, :].astype(BF16), spread)
        for j in range(4):
            to_positions(coarse_rows, k * 4 + j, up[:, j * 128 : (j + 1) * 128])
    k_near[1, z] = dot_t(eye[:16], coarse_rows[...]).astype(BF16)
    for j in (4, 3, 5, 2, 6, 1, 7):
        kz_copy(z_at(j), z).start()

    relay_frames([0, 1, 2])
    for i in (4, 5, 6, 7):
        ring_wait(n_ring, i)
    spread_frames([5, 6, 7])
    relay_frames([3, 4])
    patches[...] = (
        signal_coef * coarse_rows[...].astype(F32) + noise_coef * noise_rows[...].astype(F32)
    ).astype(BF16)

    for j in (1, 3, 2):
        px_copy(x, x_at(j)).wait_recv()
    bands = [o_bands[j].astype(F32) for j in range(4)]
    for j in range(HD // 128):
        o_all[y, core, :, j * 128 : (j + 1) * 128] = jnp.concatenate(
            [band[j * 24 : (j + 1) * 24] for band in bands], axis=0
        ).astype(BF16)
    for i in range(4):
        ring_send(o_ring, i)
    od_copy(y, core).start()

    for j in (1, 7, 2, 6, 3, 5, 4):
        kz_copy(z, z_at(j)).wait_recv()
    kx_copy(0, 0).start()
    kx_copy(1, 0).start()

    @pl.when(owner)
    def _():
        loop(1, N_Y, lambda j: y_copy(y_peer(j), y_peer(j)).wait_recv())
        cols = w_cols[...].reshape(D, 128)
        for c in (0, 1):
            both = dot(factors[c], cols)
            m_own[c] = (both[:ROWS] + both[ROWS:]).astype(BF16)

        def send_m(i):
            at_core, at_sp = m_target(i)

            @pl.when(jnp.logical_or(at_core != core, at_sp != s))
            def _():
                m_copy(i, block).start()

        loop(0, 2 * FH, send_m)
        m_all[block, pl.ds(0, ROWS), :] = m_own[core]

    relay_frames([5, 6, 7])

    kx_copy(0, 0).wait_recv()
    kx_copy(1, 0).wait_recv()
    kx_copy(0, 1).start()
    kx_copy(1, 1).start()

    natural = dot(perm[...], patches[...]).astype(BF16)
    for j in range(6):
        cols = slice(j * 256, (j + 1) * 256)
        hidden[:, cols] = dot(natural, padded_embed[:, cols]).astype(BF16)

    for i in range(4):
        ring_wait(o_ring, i)
    for i in (4, 5, 6, 7):
        ring_send(o_ring, i)
    for j in (1, -1, 2, -2):
        od_copy(y_at(j), core).start()

    def wait_m(b):
        @pl.when(not_here(b, half))
        def _():
            m_copy(core * 16 + place, b).wait_recv()

    def turn_m(blocks):
        for b in blocks:
            m_turned[b * 128 : (b + 1) * 128, :] = dot_t(eye, m_all[b])[:, :ROWS].astype(BF16)

    def frame_entries(coarse, noise):
        coarse = coarse.astype(F32)
        noise = noise.astype(F32)
        up = jnp.concatenate([coarse] * 4, axis=0)
        patch = (signal_coef * up + noise_coef * noise).astype(BF16)
        wide = patch.astype(F32)
        turned = dot(cov[...], patch)
        var = jnp.sum(wide * (turned[:64] + turned[64:128] + turned[128:]), axis=0, keepdims=True)
        wide = wide * lax.rsqrt(jnp.maximum(var, 0.0) + epsilon)
        return wide, jnp.concatenate([wide.astype(BF16), ones_row], axis=0)

    loop(0, 2 * PAIRS, wait_m)
    turn_m(range(2 * PAIRS))
    own = frame_entries(k_near[1, z], n_near[1, z])[1]
    for j in range(PAIRS):
        rows = slice(j * 128, (j + 1) * 128)
        q = dot(m_turned[rows, :], own).reshape(2, HEAD, TOKENS)
        level = jnp.sum(q * q, axis=1, keepdims=True) * (1.0 / HEAD) + epsilon
        q = (q * lax.rsqrt(level)).reshape(128, TOKENS)
        gain = jnp.concatenate([gains_turned[rows]] * 4, axis=1)
        query[rows, :] = q * gain

    ends = [clip_ref[0, 0]]
    for j in (1, 2, 3):
        ends.append(ends[-1] + clip_ref[0, j])
    first = jnp.int32(0)
    last = ends[0]
    for j in (1, 2, 3):
        inside = s >= ends[j - 1]
        first = jnp.where(inside, ends[j - 1], first)
        last = jnp.where(inside, ends[j], last)
    base = jnp.minimum(first, N_SP - WINDOW)

    near = jnp.minimum(jnp.maximum(s - base - WINDOW // 4, 0), WINDOW // 2)

    def frame_at(j):
        return base + jnp.bitwise_and(near + j, WINDOW - 1)

    def entries_at(j, far):
        t = frame_at(j)
        at_z = jnp.bitwise_and(t, 7)
        row = jnp.right_shift(t, 3) - x + 1
        near_row = jnp.minimum(jnp.maximum(row, 0), 2)
        coarse = k_near[near_row, at_z]
        noise = n_near[near_row, at_z]
        if far:
            inside = row == near_row
            coarse = jnp.where(inside, coarse, k_far[at_z])
            noise = jnp.where(inside, noise, n_far[at_z])
        wide, entries = frame_entries(coarse, noise)
        z_wide[j] = wide
        return entries

    def keys_of(entries, buffer, part):
        rows = slice(part * 256, (part + 1) * 256)
        buffer[rows, :] = dot(m_turned[HD + part * 256 : HD + (part + 1) * 256, :], entries)

    def score(j, buffer, part):
        for h in range(part * 4, part * 4 + 4):
            k = buffer[h * HEAD : (h + 1) * HEAD, :]
            q = query[h * HEAD : (h + 1) * HEAD, :]
            dots[j, h] = jnp.sum((k * q).reshape(8, 8, TOKENS), axis=0)
            squares[j, h] = jnp.sum((k * k).reshape(8, 8, TOKENS), axis=0)

    def step(j, buffer, following, other, far):
        entries = entries_at(following, far)
        for part in range(3):
            keys_of(entries, other, part)
            score(j, buffer, part)

    def start(j, far):
        entries = entries_at(j, far)
        for part in range(3):
            keys_of(entries, keys_a, part)

    def two_frames(far):
        def body(j):
            step(2 * j, keys_a, 2 * j + 1, keys_b, far)
            step(2 * j + 1, keys_b, after(2 * j + 2), keys_a, far)

        return body

    def after(j):
        return jnp.where(j == WINDOW // 2, j - 1, jnp.minimum(j, WINDOW - 1))

    start(0, False)
    loop(0, WINDOW // 4, two_frames(False))
    kx_copy(0, 1).wait_recv()
    kx_copy(1, 1).wait_recv()
    for i in range(8):
        nr_copy(i).wait_recv()
    start(WINDOW // 2, True)
    loop(WINDOW // 4, WINDOW // 2, two_frames(True))
    for i in (4, 5, 6, 7):
        ring_wait(o_ring, i)
    for j in (3, -3, 4):
        od_copy(y_at(j), core).start()
    loop(2 * PAIRS, BLOCKS, wait_m)
    turn_m(range(2 * PAIRS, BLOCKS))
    def reduce_frame(j):
        scale = lax.rsqrt(jnp.sum(squares[j], axis=1) * (1.0 / HEAD) + epsilon)
        t = frame_at(j)
        valid = jnp.logical_and(t >= first, t < last)
        probs[j] = jnp.where(valid, jnp.sum(dots[j], axis=1) * scale, -1e30)

    loop(0, WINDOW, reduce_frame)
    expo = jnp.exp(probs[...] - jnp.max(probs[...], axis=0, keepdims=True))
    probs[...] = expo / jnp.sum(expo, axis=0, keepdims=True)

    def head(h):
        total = jnp.zeros((HEAD, TOKENS), F32)
        for j in range(WINDOW):
            total = total + probs[j, pl.ds(h, 1), :] * z_wide[j]
        blended[h, pl.ds(0, 64), :] = total.astype(BF16)

    loop(0, HEADS, head)
    for h in range(HEADS):
        rows = slice(h * HEAD, (h + 1) * HEAD)
        mixed_turned[rows, :] = dot(
            m_turned[2 * HD + h * HEAD : 2 * HD + (h + 1) * HEAD, :], blended[h]
        ).astype(BF16)

    loop(0, N_Y, lambda j: od_copy(j, 1 - core).wait_recv())
    for j in range(3):
        cols = slice(j * 256, (j + 1) * 256)
        mixed[:, cols] = dot_t(perm[...], mixed_turned[cols, :]).astype(BF16)
    stores = []
    for j in range(4):
        cols = slice(j * 384, (j + 1) * 384)
        attn = dot_t(mixed[...], o_all[2 * j : 2 * j + 2].reshape(384, HD))
        result[:, cols] = (hidden[:, cols].astype(F32) + attn).astype(BF16)
        stores.append(
            pltpu.make_async_copy(result.at[:, cols], out_ref.at[:, cols], out_s.at[j])
        )
        stores[-1].start()

    for store in stores:
        store.wait()
    loop(1, N_GRP, lambda j: c_copy(grp_peer(j), g).wait_send())

    def end_w(m):
        b = m // 2
        part = lax.rem(m, 2)

        @pl.when(not_here(b, part))
        def _():
            w_copy(b, part, plane).wait_send()

    loop(0, 2 * BLOCKS, end_w)
    for copy in d_copies():
        copy.wait_send()

    @pl.when(owner)
    def _():
        loop(1, N_Y, lambda j: y_copy(y_peer(j), y).wait_send())

        def end_m(i):
            at_core, at_sp = m_target(i)

            @pl.when(jnp.logical_or(at_core != core, at_sp != s))
            def _():
                m_copy(i, block).wait_send()

        loop(0, 2 * FH, end_m)

    for j in range(1, 8):
        pz_copy(z_at(j), z).wait_send()
    for j in (1, 2, 3):
        px_copy(x_at(j), x).wait_send()
    loop(0, N_Y, lambda j: od_copy(j, core).wait_send())
    for i in range(8):
        ring_end(n_ring, i)
        ring_end(o_ring, i)
        nx_copy(0, i).wait_send()
        nx_copy(1, i).wait_send()
        nr_copy(i).wait_send()
    for j in range(1, 8):
        kz_copy(z_at(j), z).wait_send()
    kx_copy(0, 0).wait_send()
    kx_copy(1, 0).wait_send()
    kx_copy(0, 1).wait_send()
    kx_copy(1, 1).wait_send()


def local(
    coarse_latent,
    renoise,
    clip_frames,
    patch_embed,
    mod_shift,
    mod_scale,
    qkv_weight,
    out_weight,
    q_gain,
    k_gain,
):
    dma = pltpu.SemaphoreType.DMA
    sems = [10, 4, 16, 16, 36, 64, 8, 8, 2, 2, 32, 18, 8, 8, 4, 4, 8, 8, 8, 8] + [(2, 2)] * 2 + [8] * 6
    rings = [(2, 8)] * 2
    args = (
        coarse_latent.transpose(1, 2, 0, 3).reshape(N_GRP, FW * C),
        renoise,
        clip_frames,
        patch_embed,
        mod_shift,
        mod_scale,
        qkv_weight,
        out_weight,
        q_gain,
        k_gain,
    )
    inputs = [
        (pltpu.SMEM if a.dtype == jnp.int32 else pltpu.VMEM)(a.shape, a.dtype) for a in args
    ]
    return pl.pallas_call(
        kernel,
        out_shape=jax.ShapeDtypeStruct((TOKENS, D), BF16),
        in_specs=[pl.BlockSpec(memory_space=pltpu.HBM)] * len(args),
        out_specs=pl.BlockSpec(memory_space=pltpu.HBM),
        scratch_shapes=inputs
        + [
            pltpu.VMEM((N_GRP, 8, 128), F32),
            pltpu.VMEM((N_GRP, 8, 128), F32),
            pltpu.VMEM((16, 3 * HD), BF16),
            pltpu.VMEM((32, 128), F32),
            pltpu.VMEM((32, 128), BF16),
            pltpu.VMEM((2 * N_SP, 16, 128), BF16),
            pltpu.VMEM((N_Y, 2 * PLANE_ROWS, 128), BF16),
            pltpu.VMEM((1, D), F32),
            pltpu.VMEM((1, D), F32),
            pltpu.VMEM((2, 2 * ROWS, D), BF16),
            pltpu.VMEM((2, ROWS, 128), BF16),
            pltpu.VMEM((BLOCKS, 128, 128), BF16),
            pltpu.VMEM((3 * HD, ROWS), BF16),
            pltpu.VMEM((TOKENS, 128), BF16),
            pltpu.VMEM((TOKENS, 128), BF16),
            pltpu.VMEM((TOKENS, 128), BF16),
            pltpu.VMEM((192, 64), BF16),
            pltpu.VMEM((3, 8, 64, TOKENS), BF16),
            pltpu.VMEM((8, 64, TOKENS), BF16),
            pltpu.VMEM((3, 8, 16, TOKENS), BF16),
            pltpu.VMEM((8, 16, TOKENS), BF16),
            pltpu.VMEM((WINDOW, HEAD, TOKENS), F32),
            pltpu.VMEM((8, 32, 128), BF16),
            pltpu.VMEM((144, 128), BF16),
            pltpu.VMEM((4, 144, 128), BF16),
            pltpu.VMEM((N_Y, 2, PLANE_ROWS, HD), BF16),
            pltpu.VMEM((TOKENS, TOKENS), BF16),
            pltpu.VMEM((HD, TOKENS), F32),
            pltpu.VMEM((HD, TOKENS), F32),
            pltpu.VMEM((HD, TOKENS), F32),
            pltpu.VMEM((WINDOW, HEADS, 8, TOKENS), F32),
            pltpu.VMEM((WINDOW, HEADS, 8, TOKENS), F32),
            pltpu.VMEM((WINDOW, HEADS, TOKENS), F32),
            pltpu.VMEM((HEADS, ROWS, TOKENS), BF16),
            pltpu.VMEM((HD, TOKENS), BF16),
            pltpu.VMEM((TOKENS, HD), BF16),
            pltpu.VMEM((128, D), BF16),
            pltpu.VMEM((TOKENS, D), BF16),
            pltpu.VMEM((TOKENS, D), BF16),
        ]
        + [dma(n if isinstance(n, tuple) else (n,)) for n in sems]
        + [dma(n) for n in rings],
        compiler_params=pltpu.CompilerParams(
            collective_id=0, has_side_effects=True, vmem_limit_bytes=63 * 1024 * 1024
        ),
    )(*args)


def solution(mesh):
    placed = (
        P(None, "sp", "grp", None),
        P(("grp", "sp"), None),
        P("grp", None),
        P(),
        P("grp", None),
        P("grp", None),
        P(("grp", "sp"), None),
        P(("grp", "sp"), None),
        P(),
        P(),
    )
    return jax.shard_map(
        local, mesh=mesh, in_specs=placed, out_specs=P(("grp", "sp"), None), check_vma=False
    )
```

```python
import jax
import jax.numpy as jnp
from jax import lax
from jax.experimental import pallas as pl
from jax.experimental.pallas import tpu as pltpu
from jax.sharding import PartitionSpec as P

HEADS = 12
HEAD = 64
C = 16
FH = 16
FW = 32
D = 1536
HD = HEADS * HEAD
TOKENS = FH * FW
WINDOW = 16
N_GRP = 16
N_Y = 8
N_SP = 32
BLOCKS = 3 * HD // 128
PAIRS = HEADS // 2
ROWS = 80
PLANE_ROWS = 96

signal_coef = 0.8
noise_coef = 0.6
epsilon = 1e-06
MESH = pl.DeviceIdType.MESH
F32 = jnp.float32
BF16 = jnp.bfloat16


def iota(shape, axis):
    return lax.broadcasted_iota(jnp.int32, shape, axis)


def dot(a, b):
    return jnp.dot(a, b, preferred_element_type=F32)


def dot_t(a, b):
    return lax.dot_general(a, b, (((1,), (1,)), ((), ())), preferred_element_type=F32)


def one_hot(condition):
    return jnp.where(condition, 1.0, 0.0).astype(BF16)


def kernel(
    coarse_any,
    noise_any,
    clip_any,
    embed_any,
    shift_any,
    scale_any,
    w_any,
    o_any,
    qg_any,
    kg_any,
    out_ref,
    coarse_in,
    noise_ref,
    clip_ref,
    embed_ref,
    shift_ref,
    scale_ref,
    w_in,
    o_in,
    qg_ref,
    kg_ref,
    c_send,
    c_recv,
    w_ref,
    o_wide,
    o_ref,
    w_tiles,
    w_cols,
    sibling_scale,
    sibling_shift,
    factors,
    m_own,
    m_all,
    m_turned,
    patches,
    noise_rows,
    coarse_rows,
    cov,
    n_near,
    n_far,
    k_near,
    k_far,
    z_wide,
    o_tiles,
    o_own,
    o_bands,
    o_all,
    perm,
    query,
    keys_a,
    keys_b,
    dots,
    squares,
    probs,
    blended,
    mixed_turned,
    mixed,
    padded_embed,
    hidden,
    result,
    in_s,
    out_s,
    c_ss,
    c_rs,
    w_ss,
    w_rs,
    y_ss,
    y_rs,
    d_ss,
    d_rs,
    m_ss,
    m_rs,
    pz_ss,
    pz_rs,
    px_ss,
    px_rs,
    od_ss,
    od_rs,
    kz_ss,
    kz_rs,
    kx_ss,
    kx_rs,
    o2_ss,
    o2_rs,
    n2_ss,
    n2_rs,
    nr_ss,
    nr_rs,
    nx_ss,
    nx_rs,
):
    g = lax.axis_index("grp")
    s = lax.axis_index("sp")
    y = g // 2
    core = lax.rem(g, 2)
    sibling = g + 1 - 2 * core
    x = s // 8
    z = lax.rem(s, 8)
    half = z // 4
    place = x * 4 + lax.rem(z, 4)
    first_pick = lax.rem(place, 2) == core
    owner = jnp.logical_or(first_pick, jnp.logical_or(place == 12, place == 13))
    block = jnp.where(first_pick, place, place + 4)
    plane = core * N_SP + s

    def sp_peer(j):
        return lax.rem(s + j, N_SP)

    def grp_peer(j):
        return lax.rem(g + j, N_GRP)

    def y_peer(j):
        return lax.rem(y + j, N_Y)

    def x_at(j):
        return lax.rem(x + j + 4, 4)

    def z_at(j):
        return lax.rem(z + j + 8, 8)

    def owner_core(b):
        return jnp.where(b < 16, lax.rem(b, 2), 1 - lax.rem(b, 2))

    def owner_sp(b, part):
        q = jnp.where(b < 16, b, b - 4)
        return (q // 4) * 8 + part * 4 + lax.rem(q, 4)

    def not_here(b, part):
        return jnp.logical_or(owner_core(b) != core, owner_sp(b, part) != s)

    def remote(src, dst, send_sem, recv_sem, to):
        return pltpu.make_async_remote_copy(
            src_ref=src,
            dst_ref=dst,
            send_sem=send_sem,
            recv_sem=recv_sem,
            device_id=to,
            device_id_type=MESH,
        )

    def loop(start, stop, body):
        def step(j, carry):
            body(j)
            return carry

        lax.fori_loop(start, stop, step, 0)

    def c_copy(to, slot):
        return remote(
            c_send.at[to], c_recv.at[slot], c_ss.at[to], c_rs.at[slot], (to, s)
        )

    def w_copy(b, part, slot):
        return remote(
            w_ref.at[:, pl.ds(pl.multiple_of(b * 128, 128), 128)],
            w_tiles.at[slot],
            w_ss.at[2 * b + part],
            w_rs.at[slot],
            (2 * y + owner_core(b), owner_sp(b, part)),
        )

    def y_copy(to, slot):
        return remote(
            w_cols.at[y], w_cols.at[slot], y_ss.at[to], y_rs.at[slot], (2 * to + core, s)
        )

    def d_copies():
        to = (sibling, s)
        return [
            remote(scale_ref, sibling_scale, d_ss.at[0], d_rs.at[0], to),
            remote(shift_ref, sibling_shift, d_ss.at[1], d_rs.at[1], to),
        ]

    def m_target(i):
        return i // 16, (lax.rem(i, 16) // 4) * 8 + half * 4 + lax.rem(i, 4)

    def m_copy(i, b):
        at_core, at_sp = m_target(i)
        return remote(
            m_own.at[at_core],
            m_all.at[b, pl.ds(0, ROWS)],
            m_ss.at[i],
            m_rs.at[b],
            (2 * y + at_core, at_sp),
        )

    def pz_copy(to, slot):
        return remote(o_ref, o_tiles.at[slot], pz_ss.at[to], pz_rs.at[slot], (g, x * 8 + to))

    def px_copy(to, slot):
        return remote(o_own, o_bands.at[slot], px_ss.at[to], px_rs.at[slot], (g, to * 8 + z))

    def od_copy(slot, half):
        return remote(
            o_all.at[slot, half], o_all.at[slot, half], od_ss.at[slot], od_rs.at[slot], (sibling, s)
        )

    def kz_copy(to, slot):
        part = k_near.at[1, slot]
        return remote(part, part, kz_ss.at[to], kz_rs.at[slot], (g, x * 8 + to))

    def kx_copy(way, k):
        if k == 0:
            src, dst = k_near.at[1], k_near.at[2 * way]
        else:
            half_row = pl.ds(4 * way, 4)
            src, dst = k_near.at[2 * way, half_row], k_far.at[half_row]
        to = x_at(1) if way == 0 else x_at(-1)
        return remote(src, dst, kx_ss.at[way, k], kx_rs.at[way, k], (g, to * 8 + z))

    moves = [(1, 0, 0), (-1, 0, 0), (2, 0, 0), (-2, 0, 0), (1, -2, 0), (-1, 2, 0), (2, -2, 1), (-2, 2, 2)]

    def ring_copy(view, at, to, sems, i, start):
        part = view(at(start), moves[i][2])
        return remote(part, part, sems[0].at[i], sems[1].at[i], to(at(moves[i][0])))

    def ring_send(ring, i):
        ring_copy(*ring, i, moves[i][1]).start()

    def ring_wait(ring, i):
        ring_copy(*ring, i, moves[i][1] - moves[i][0]).wait_recv()

    def ring_end(ring, i):
        ring_copy(*ring, i, moves[i][1]).wait_send()

    def o_view(slot, part):
        rows = (pl.ds(0, PLANE_ROWS), pl.ds(0, 48), pl.ds(48, 48))[part]
        return o_all.at[slot, core, rows]

    def n_view(slot, part):
        rows = (pl.ds(0, 64), pl.ds(0, 32), pl.ds(32, 32))[part]
        return n_near.at[1, slot, rows]

    def y_at(j):
        return lax.rem(y + j + N_Y, N_Y)

    o_ring = (o_view, y_at, lambda to: (2 * to + core, s), (o2_ss, o2_rs))
    n_ring = (n_view, z_at, lambda to: (g, x * 8 + to), (n2_ss, n2_rs))

    offsets = [0, -1, 1, -2, 2, -3, 3, -4]

    def nx_copy(way, i):
        slot = z_at(offsets[i])
        to = x_at(1) if way == 0 else x_at(-1)
        return remote(
            n_near.at[1, slot],
            n_near.at[2 * way, slot],
            nx_ss.at[way, i],
            nx_rs.at[way, i],
            (g, to * 8 + z),
        )

    def nr_copy(i):
        slot = z_at(offsets[i])
        way = i % 2
        to = x_at(1) if way == 0 else x_at(-1)
        return remote(
            n_near.at[2 * way, slot], n_far.at[slot], nr_ss.at[i], nr_rs.at[i], (g, to * 8 + z)
        )

    def spread_frames(indices):
        for i in indices:
            nx_copy(0, i).start()
            nx_copy(1, i).start()

    def relay_frames(indices):
        for i in indices:
            nx_copy(0, i).wait_recv()
            nx_copy(1, i).wait_recv()
            nr_copy(i).start()

    pairs = [
        (w_any, w_in),
        (coarse_any, coarse_in),
        (o_any, o_in),
        (noise_any, noise_ref),
        (scale_any, scale_ref),
        (shift_any, shift_ref),
        (embed_any, embed_ref),
        (clip_any, clip_ref),
        (qg_any, qg_ref),
        (kg_any, kg_ref),
    ]
    loads = [pltpu.make_async_copy(a, b, in_s.at[i]) for i, (a, b) in enumerate(pairs)]
    for load in loads:
        load.start()

    barrier = pltpu.get_barrier_semaphore()

    def greet_plane(j):
        other = lax.rem(plane + j, 2 * N_SP)
        pl.semaphore_signal(
            barrier,
            inc=1,
            device_id=(2 * y + other // N_SP, lax.rem(other, N_SP)),
            device_id_type=MESH,
        )

    def greet_y(j):
        for c in (0, 1):
            pl.semaphore_signal(
                barrier, inc=1, device_id=(2 * y_peer(j) + c, s), device_id_type=MESH
            )

    loop(1, 2 * N_SP, greet_plane)
    loop(1, N_Y, greet_y)

    w_ref[...] = jnp.zeros((16, 3 * HD), BF16)
    o_wide[...] = jnp.zeros((32, 128), F32)
    for load in loads[:6]:
        load.wait()
    w_ref[0:3, :] = w_in[...]
    coarse = coarse_in[...].astype(F32)
    for k in range(4):
        c_send[:, k, :] = coarse[:, k * 128 : (k + 1) * 128]
    o_rows = o_in[...].astype(F32)
    for j in range(6):
        o_wide[4 * j : 4 * j + 3, :] = o_rows[:, j * 128 : (j + 1) * 128]
    o_ref[...] = o_wide[...].astype(BF16)

    lane = iota((FH, 128), 1)
    eye = one_hot(iota((128, 128), 0) == iota((128, 128), 1))

    def to_positions(ref, k, piece):
        ref[2 * k * FH : (2 * k + 1) * FH, :] = jnp.where(lane < 64, piece, 0.0).astype(BF16)
        ref[(2 * k + 1) * FH : (2 * k + 2) * FH, :] = jnp.where(
            lane < 64, pltpu.roll(piece, 64, 1), 0.0
        ).astype(BF16)

    for k in range(16):
        to_positions(noise_rows, k, noise_ref[:, k * 128 : (k + 1) * 128].astype(F32))
    n_near[1, z] = dot_t(eye[:64], noise_rows[...]).astype(BF16)

    pl.semaphore_wait(barrier, 2 * N_SP - 1 + 2 * (N_Y - 1))

    loop(1, N_GRP, lambda j: c_copy(grp_peer(j), g).start())
    c_recv[g] = c_send[g]
    for copy in d_copies():
        copy.start()

    def send_w(j):
        m = lax.rem(j + 4 * place, 2 * BLOCKS)
        b = m // 2
        part = lax.rem(m, 2)

        @pl.when(not_here(b, part))
        def _():
            w_copy(b, part, plane).start()

    for i in range(4):
        ring_send(n_ring, i)
    spread_frames([0])
    loop(0, 2 * BLOCKS, send_w)

    @pl.when(owner)
    def _():
        w_tiles[plane] = w_ref[:, pl.ds(pl.multiple_of(block * 128, 128), 128)]

    for j in (4, 3, 5, 2, 6, 1, 7):
        pz_copy(z_at(j), z).start()
    o_tiles[z] = o_ref[...]

    for load in loads[6:]:
        load.wait()
    embed = embed_ref[...].astype(F32)
    centered = embed - jnp.mean(embed, axis=1, keepdims=True)
    away_hi = centered.astype(BF16)
    away = jnp.concatenate([away_hi, (centered - away_hi.astype(F32)).astype(BF16)], axis=0)
    gram = dot_t(away, away) * (1.0 / D)
    gram = gram[:64] + gram[64:]
    gram = (gram + pltpu.roll(gram, 64, 1))[:, :64]
    for j in range(3):
        part = gram.astype(BF16)
        cov[j * 64 : (j + 1) * 64, :] = part
        gram = gram - part.astype(F32)

    def set_factors(at, scale, shift):
        scaled = centered * scale
        scaled_hi = scaled.astype(BF16)
        shift = jnp.where(iota((16, D), 0) == 0, jnp.broadcast_to(shift, (16, D)), 0.0)
        shift_hi = shift.astype(BF16)
        factors[at, pl.ds(0, 64), :] = scaled_hi
        factors[at, pl.ds(64, 16), :] = shift_hi
        factors[at, pl.ds(ROWS, 64), :] = (scaled - scaled_hi.astype(F32)).astype(BF16)
        factors[at, pl.ds(ROWS + 64, 16), :] = (shift - shift_hi.astype(F32)).astype(BF16)

    for copy in d_copies():
        copy.wait_recv()

    @pl.when(owner)
    def _():
        set_factors(core, scale_ref[...], shift_ref[...])
        set_factors(1 - core, sibling_scale[...], sibling_shift[...])

    padded_embed[pl.ds(0, 64), :] = embed_ref[...]
    padded_embed[pl.ds(64, 64), :] = jnp.zeros((64, D), BF16)
    gains = qg_ref[...] * kg_ref[...] * (1.0 / 8.0)
    gains_turned = jnp.broadcast_to(gains.reshape(1, HD), (128, HD)).T

    def fill_perm(j):
        base = pl.multiple_of(j * 64, 64)
        row = iota((64, TOKENS), 0) + base
        col = iota((64, TOKENS), 1)
        same = jnp.logical_and(
            jnp.right_shift(row, 5) == jnp.bitwise_and(col, 15),
            jnp.bitwise_and(row, 31) == jnp.right_shift(col, 4),
        )
        perm[pl.ds(base, 64), :] = one_hot(same)

    loop(0, TOKENS // 64, fill_perm)

    def pad_m(j):
        m_all[j, pl.ds(ROWS, 128 - ROWS), :] = jnp.zeros((128 - ROWS, 128), BF16)

    loop(0, BLOCKS, pad_m)
    ones_row = one_hot(iota((16, TOKENS), 0) == 0)

    def pad_blended(j):
        blended[j, pl.ds(64, 16), :] = ones_row

    loop(0, HEADS, pad_blended)


    for i in (0, 1):
        ring_wait(n_ring, i)
    spread_frames([1, 2])
    for i in (2, 3):
        ring_wait(n_ring, i)
    for i in (4, 5, 6, 7):
        ring_send(n_ring, i)
    spread_frames([3, 4])

    @pl.when(owner)
    def _():
        def wait_w(j):
            w_copy(block, half, lax.rem(plane + j, 2 * N_SP)).wait_recv()

        loop(1, 2 * N_SP, wait_w)
        row = iota((2 * PLANE_ROWS, 1024), 0)
        col = iota((2 * PLANE_ROWS, 1024), 1)
        within = jnp.bitwise_and(col, 15)
        pick = one_hot(
            jnp.logical_and(within < 3, row == jnp.right_shift(col, 4) * 3 + within)
        )
        w_cols[y] = dot(pick, w_tiles[...].reshape(1024, 128)).astype(BF16)
        loop(1, N_Y, lambda j: y_copy(y_peer(j), y).start())

    for j in (1, 7, 2, 6, 3, 5, 4):
        pz_copy(z, z_at(j)).wait_recv()
    row = iota((144, 256), 0)
    col = iota((144, 256), 1)
    third = jnp.bitwise_and(col, 3)
    column = jnp.right_shift(jnp.bitwise_and(col, 31), 2)
    pick_rows = one_hot(
        jnp.logical_and(third < 3, row == column * 24 + jnp.right_shift(col, 5) * 3 + third)
    )
    o_own[...] = dot(pick_rows, o_tiles[...].reshape(256, 128)).astype(BF16)
    for j in (2, 1, 3):
        px_copy(x_at(j), x).start()
    o_bands[x] = o_own[...]

    spread_row = iota((128, 512), 0)
    spread_col = iota((128, 512), 1)
    spread = one_hot(
        jnp.logical_and(
            jnp.right_shift(spread_row, 4) == jnp.right_shift(spread_col, 6),
            jnp.bitwise_and(spread_row, 15) == jnp.bitwise_and(spread_col, 15),
        )
    )

    def wait_c(j):
        c_copy(grp_peer(j), grp_peer(j)).wait_recv()

    loop(1, N_GRP, wait_c)
    for k in range(4):
        up = dot(c_recv[:, k, :].astype(BF16), spread)
        for j in range(4):
            to_positions(coarse_rows, k * 4 + j, up[:, j * 128 : (j + 1) * 128])
    k_near[1, z] = dot_t(eye[:16], coarse_rows[...]).astype(BF16)
    for j in (4, 3, 5, 2, 6, 1, 7):
        kz_copy(z_at(j), z).start()

    relay_frames([0, 1, 2])
    for i in (4, 5, 6, 7):
        ring_wait(n_ring, i)
    spread_frames([5, 6, 7])
    relay_frames([3, 4])
    patches[...] = (
        signal_coef * coarse_rows[...].astype(F32) + noise_coef * noise_rows[...].astype(F32)
    ).astype(BF16)

    for j in (1, 3, 2):
        px_copy(x, x_at(j)).wait_recv()
    bands = [o_bands[j].astype(F32) for j in range(4)]
    for j in range(HD // 128):
        o_all[y, core, :, j * 128 : (j + 1) * 128] = jnp.concatenate(
            [band[j * 24 : (j + 1) * 24] for band in bands], axis=0
        ).astype(BF16)
    for i in range(4):
        ring_send(o_ring, i)
    od_copy(y, core).start()

    for j in (1, 7, 2, 6, 3, 5, 4):
        kz_copy(z, z_at(j)).wait_recv()
    kx_copy(0, 0).start()
    kx_copy(1, 0).start()

    @pl.when(owner)
    def _():
        loop(1, N_Y, lambda j: y_copy(y_peer(j), y_peer(j)).wait_recv())
        cols = w_cols[...].reshape(D, 128)
        for c in (0, 1):
            both = dot(factors[c], cols)
            m_own[c] = (both[:ROWS] + both[ROWS:]).astype(BF16)

        def send_m(i):
            at_core, at_sp = m_target(i)

            @pl.when(jnp.logical_or(at_core != core, at_sp != s))
            def _():
                m_copy(i, block).start()

        loop(0, 2 * FH, send_m)
        m_all[block, pl.ds(0, ROWS), :] = m_own[core]

    relay_frames([5, 6, 7])

    kx_copy(0, 0).wait_recv()
    kx_copy(1, 0).wait_recv()
    kx_copy(0, 1).start()
    kx_copy(1, 1).start()

    for i in range(4):
        ring_wait(o_ring, i)
    for i in (4, 5, 6, 7):
        ring_send(o_ring, i)
    for j in (1, -1, 2, -2):
        od_copy(y_at(j), core).start()

    natural = dot(perm[...], patches[...]).astype(BF16)
    for j in range(6):
        cols = slice(j * 256, (j + 1) * 256)
        hidden[:, cols] = dot(natural, padded_embed[:, cols]).astype(BF16)

    def wait_m(b):
        @pl.when(not_here(b, half))
        def _():
            m_copy(core * 16 + place, b).wait_recv()

    def turn_m(blocks):
        for b in blocks:
            m_turned[b * 128 : (b + 1) * 128, :] = dot_t(eye, m_all[b])[:, :ROWS].astype(BF16)

    def frame_entries(coarse, noise):
        coarse = coarse.astype(F32)
        noise = noise.astype(F32)
        up = jnp.concatenate([coarse] * 4, axis=0)
        patch = (signal_coef * up + noise_coef * noise).astype(BF16)
        wide = patch.astype(F32)
        turned = dot(cov[...], patch)
        var = jnp.sum(wide * (turned[:64] + turned[64:128] + turned[128:]), axis=0, keepdims=True)
        wide = wide * lax.rsqrt(jnp.maximum(var, 0.0) + epsilon)
        return wide, jnp.concatenate([wide.astype(BF16), ones_row], axis=0)

    loop(0, 2 * PAIRS, wait_m)
    turn_m(range(2 * PAIRS))
    own = frame_entries(k_near[1, z], n_near[1, z])[1]
    for j in range(PAIRS):
        rows = slice(j * 128, (j + 1) * 128)
        q = dot(m_turned[rows, :], own).reshape(2, HEAD, TOKENS)
        level = jnp.sum(q * q, axis=1, keepdims=True) * (1.0 / HEAD) + epsilon
        q = (q * lax.rsqrt(level)).reshape(128, TOKENS)
        gain = jnp.concatenate([gains_turned[rows]] * 4, axis=1)
        query[rows, :] = q * gain

    ends = [clip_ref[0, 0]]
    for j in (1, 2, 3):
        ends.append(ends[-1] + clip_ref[0, j])
    first = jnp.int32(0)
    last = ends[0]
    for j in (1, 2, 3):
        inside = s >= ends[j - 1]
        first = jnp.where(inside, ends[j - 1], first)
        last = jnp.where(inside, ends[j], last)
    base = jnp.minimum(first, N_SP - WINDOW)

    near = jnp.minimum(jnp.maximum(s - base - WINDOW // 4, 0), WINDOW // 2)

    def frame_at(j):
        return base + jnp.bitwise_and(near + j, WINDOW - 1)

    def entries_at(j, far):
        t = frame_at(j)
        at_z = jnp.bitwise_and(t, 7)
        row = jnp.right_shift(t, 3) - x + 1
        near_row = jnp.minimum(jnp.maximum(row, 0), 2)
        coarse = k_near[near_row, at_z]
        noise = n_near[near_row, at_z]
        if far:
            inside = row == near_row
            coarse = jnp.where(inside, coarse, k_far[at_z])
            noise = jnp.where(inside, noise, n_far[at_z])
        wide, entries = frame_entries(coarse, noise)
        z_wide[j] = wide
        return entries

    def keys_of(entries, buffer, part):
        rows = slice(part * 256, (part + 1) * 256)
        buffer[rows, :] = dot(m_turned[HD + part * 256 : HD + (part + 1) * 256, :], entries)

    def score(j, buffer, part):
        for h in range(part * 4, part * 4 + 4):
            k = buffer[h * HEAD : (h + 1) * HEAD, :]
            q = query[h * HEAD : (h + 1) * HEAD, :]
            dots[j, h] = jnp.sum((k * q).reshape(8, 8, TOKENS), axis=0)
            squares[j, h] = jnp.sum((k * k).reshape(8, 8, TOKENS), axis=0)

    def step(j, buffer, following, other, far):
        entries = entries_at(following, far)
        for part in range(3):
            keys_of(entries, other, part)
            score(j, buffer, part)

    def start(j, far):
        entries = entries_at(j, far)
        for part in range(3):
            keys_of(entries, keys_a, part)

    def two_frames(far):
        def body(j):
            step(2 * j, keys_a, 2 * j + 1, keys_b, far)
            step(2 * j + 1, keys_b, after(2 * j + 2), keys_a, far)

        return body

    def after(j):
        return jnp.where(j == WINDOW // 2, j - 1, jnp.minimum(j, WINDOW - 1))

    start(0, False)
    loop(0, WINDOW // 4, two_frames(False))
    kx_copy(0, 1).wait_recv()
    kx_copy(1, 1).wait_recv()
    for i in range(8):
        nr_copy(i).wait_recv()
    start(WINDOW // 2, True)
    loop(WINDOW // 4, WINDOW // 2, two_frames(True))
    for i in (4, 5, 6, 7):
        ring_wait(o_ring, i)
    for j in (3, -3, 4):
        od_copy(y_at(j), core).start()
    loop(2 * PAIRS, BLOCKS, wait_m)
    turn_m(range(2 * PAIRS, BLOCKS))
    def reduce_frame(j):
        scale = lax.rsqrt(jnp.sum(squares[j], axis=1) * (1.0 / HEAD) + epsilon)
        t = frame_at(j)
        valid = jnp.logical_and(t >= first, t < last)
        probs[j] = jnp.where(valid, jnp.sum(dots[j], axis=1) * scale, -1e30)

    loop(0, WINDOW, reduce_frame)
    expo = jnp.exp(probs[...] - jnp.max(probs[...], axis=0, keepdims=True))
    probs[...] = expo / jnp.sum(expo, axis=0, keepdims=True)

    def head(h):
        total = jnp.zeros((HEAD, TOKENS), F32)
        for j in range(WINDOW):
            total = total + probs[j, pl.ds(h, 1), :] * z_wide[j]
        blended[h, pl.ds(0, 64), :] = total.astype(BF16)

    loop(0, HEADS, head)
    for h in range(HEADS):
        rows = slice(h * HEAD, (h + 1) * HEAD)
        mixed_turned[rows, :] = dot(
            m_turned[2 * HD + h * HEAD : 2 * HD + (h + 1) * HEAD, :], blended[h]
        ).astype(BF16)

    loop(0, N_Y, lambda j: od_copy(j, 1 - core).wait_recv())
    for j in range(3):
        cols = slice(j * 256, (j + 1) * 256)
        mixed[:, cols] = dot_t(perm[...], mixed_turned[cols, :]).astype(BF16)
    stores = []
    for j in range(4):
        cols = slice(j * 384, (j + 1) * 384)
        attn = dot_t(mixed[...], o_all[2 * j : 2 * j + 2].reshape(384, HD))
        result[:, cols] = (hidden[:, cols].astype(F32) + attn).astype(BF16)
        stores.append(
            pltpu.make_async_copy(result.at[:, cols], out_ref.at[:, cols], out_s.at[j])
        )
        stores[-1].start()

    for store in stores:
        store.wait()
    loop(1, N_GRP, lambda j: c_copy(grp_peer(j), g).wait_send())

    def end_w(m):
        b = m // 2
        part = lax.rem(m, 2)

        @pl.when(not_here(b, part))
        def _():
            w_copy(b, part, plane).wait_send()

    loop(0, 2 * BLOCKS, end_w)
    for copy in d_copies():
        copy.wait_send()

    @pl.when(owner)
    def _():
        loop(1, N_Y, lambda j: y_copy(y_peer(j), y).wait_send())

        def end_m(i):
            at_core, at_sp = m_target(i)

            @pl.when(jnp.logical_or(at_core != core, at_sp != s))
            def _():
                m_copy(i, block).wait_send()

        loop(0, 2 * FH, end_m)

    for j in range(1, 8):
        pz_copy(z_at(j), z).wait_send()
    for j in (1, 2, 3):
        px_copy(x_at(j), x).wait_send()
    loop(0, N_Y, lambda j: od_copy(j, core).wait_send())
    for i in range(8):
        ring_end(n_ring, i)
        ring_end(o_ring, i)
        nx_copy(0, i).wait_send()
        nx_copy(1, i).wait_send()
        nr_copy(i).wait_send()
    for j in range(1, 8):
        kz_copy(z_at(j), z).wait_send()
    kx_copy(0, 0).wait_send()
    kx_copy(1, 0).wait_send()
    kx_copy(0, 1).wait_send()
    kx_copy(1, 1).wait_send()


def local(
    coarse_latent,
    renoise,
    clip_frames,
    patch_embed,
    mod_shift,
    mod_scale,
    qkv_weight,
    out_weight,
    q_gain,
    k_gain,
):
    dma = pltpu.SemaphoreType.DMA
    sems = [10, 4, 16, 16, 36, 64, 8, 8, 2, 2, 32, 18, 8, 8, 4, 4, 8, 8, 8, 8] + [(2, 2)] * 2 + [8] * 6
    rings = [(2, 8)] * 2
    args = (
        coarse_latent.transpose(1, 2, 0, 3).reshape(N_GRP, FW * C),
        renoise,
        clip_frames,
        patch_embed,
        mod_shift,
        mod_scale,
        qkv_weight,
        out_weight,
        q_gain,
        k_gain,
    )
    inputs = [
        (pltpu.SMEM if a.dtype == jnp.int32 else pltpu.VMEM)(a.shape, a.dtype) for a in args
    ]
    return pl.pallas_call(
        kernel,
        out_shape=jax.ShapeDtypeStruct((TOKENS, D), BF16),
        in_specs=[pl.BlockSpec(memory_space=pltpu.HBM)] * len(args),
        out_specs=pl.BlockSpec(memory_space=pltpu.HBM),
        scratch_shapes=inputs
        + [
            pltpu.VMEM((N_GRP, 8, 128), F32),
            pltpu.VMEM((N_GRP, 8, 128), F32),
            pltpu.VMEM((16, 3 * HD), BF16),
            pltpu.VMEM((32, 128), F32),
            pltpu.VMEM((32, 128), BF16),
            pltpu.VMEM((2 * N_SP, 16, 128), BF16),
            pltpu.VMEM((N_Y, 2 * PLANE_ROWS, 128), BF16),
            pltpu.VMEM((1, D), F32),
            pltpu.VMEM((1, D), F32),
            pltpu.VMEM((2, 2 * ROWS, D), BF16),
            pltpu.VMEM((2, ROWS, 128), BF16),
            pltpu.VMEM((BLOCKS, 128, 128), BF16),
            pltpu.VMEM((3 * HD, ROWS), BF16),
            pltpu.VMEM((TOKENS, 128), BF16),
            pltpu.VMEM((TOKENS, 128), BF16),
            pltpu.VMEM((TOKENS, 128), BF16),
            pltpu.VMEM((192, 64), BF16),
            pltpu.VMEM((3, 8, 64, TOKENS), BF16),
            pltpu.VMEM((8, 64, TOKENS), BF16),
            pltpu.VMEM((3, 8, 16, TOKENS), BF16),
            pltpu.VMEM((8, 16, TOKENS), BF16),
            pltpu.VMEM((WINDOW, HEAD, TOKENS), F32),
            pltpu.VMEM((8, 32, 128), BF16),
            pltpu.VMEM((144, 128), BF16),
            pltpu.VMEM((4, 144, 128), BF16),
            pltpu.VMEM((N_Y, 2, PLANE_ROWS, HD), BF16),
            pltpu.VMEM((TOKENS, TOKENS), BF16),
            pltpu.VMEM((HD, TOKENS), F32),
            pltpu.VMEM((HD, TOKENS), F32),
            pltpu.VMEM((HD, TOKENS), F32),
            pltpu.VMEM((WINDOW, HEADS, 8, TOKENS), F32),
            pltpu.VMEM((WINDOW, HEADS, 8, TOKENS), F32),
            pltpu.VMEM((WINDOW, HEADS, TOKENS), F32),
            pltpu.VMEM((HEADS, ROWS, TOKENS), BF16),
            pltpu.VMEM((HD, TOKENS), BF16),
            pltpu.VMEM((TOKENS, HD), BF16),
            pltpu.VMEM((128, D), BF16),
            pltpu.VMEM((TOKENS, D), BF16),
            pltpu.VMEM((TOKENS, D), BF16),
        ]
        + [dma(n if isinstance(n, tuple) else (n,)) for n in sems]
        + [dma(n) for n in rings],
        compiler_params=pltpu.CompilerParams(
            collective_id=0, has_side_effects=True, vmem_limit_bytes=63 * 1024 * 1024
        ),
    )(*args)


def solution(mesh):
    placed = (
        P(None, "sp", "grp", None),
        P(("grp", "sp"), None),
        P("grp", None),
        P(),
        P("grp", None),
        P("grp", None),
        P(("grp", "sp"), None),
        P(("grp", "sp"), None),
        P(),
        P(),
    )
    return jax.shard_map(
        local, mesh=mesh, in_specs=placed, out_specs=P(("grp", "sp"), None), check_vma=False
    )
```
